32 devices in a mesh: seq: 8 (over z, x), head: 4 (over y, core).
Axes of the slice: x: 2, y: 2, z: 4, core: 2. Of those that a mesh axis runs over, the one named last changes fastest.
Arguments:
- queries: bfloat16 [16384, 2048], P(('seq', 'head')), may hold values from -6 to 6
- keys: bfloat16 [16384, 2048], P(('seq', 'head')), may hold values from -6 to 6
- values: bfloat16 [16384, 2048], P(('seq', 'head')), may hold values from -44.2 to 44.2
- log_decay: float32 [16384, 8], P('seq', 'head'), may hold values from -0.7 to 0
- selection: int32 [4, 3], replicated, may hold values from 0 to 3, as said below
- out_gain: float32 [2048], P('head'), may hold values from 0.5 to 1.5
Outputs:
- mixed: bfloat16 [16384, 2048], P('seq', 'head')
The draws below stay inside these ranges and needn't reach their ends.
Inputs may be any that keep to these rules, and one draw needn't show every extreme that they name: `selection`: row i begins with i; its other two entries are two different blocks before block i, or i itself where fewer than two earlier blocks exist.
All inputs are finite; a program needn't handle non-finite values.
Results may differ from the reference program's by a relative error of at most 0.0044.
Values may be sent and summed in bfloat16 or wider, within the bound.
No kernel may reach another device: no remote copies, remote signals or barrier semaphores. Data moves between devices by JAX's collectives and lax.ppermute only.
A program may use at most 128 MiB of HBM per device.

```python
import math
import jax
import jax.numpy as jnp
from jax import lax

HEADS = 16
HD = 128
TOK_DEV = 2048
BLK = 4096
TILE = 1024
CH = 128
CONTEXT_LENGTH = 16384


def draw_queries(key, part):
    own_key = jax.random.fold_in(key, 1)
    return jnp.clip(jax.random.normal(own_key, (CONTEXT_LENGTH, HEADS * HD), jnp.float32), -4.0, 4.0).astype(jnp.bfloat16)


def draw_keys(key, part):
    own_key = jax.random.fold_in(key, 2)
    return jnp.clip(jax.random.normal(own_key, (CONTEXT_LENGTH, HEADS * HD), jnp.float32), -4.0, 4.0).astype(jnp.bfloat16)


def draw_values(key, part):
    first, second, third = jax.random.split(jax.random.fold_in(key, 3), 3)
    columns = jnp.exp(jax.random.uniform(first, (1, HEADS * HD), jnp.float32, -1.2, 1.2))
    record_entries = jnp.exp(jax.random.uniform(second, (CONTEXT_LENGTH, 1), jnp.float32, -1.2, 1.2))
    core = jnp.clip(jax.random.normal(third, (CONTEXT_LENGTH, HEADS * HD), jnp.float32), -4.0, 4.0)
    return (core * columns * record_entries).astype(jnp.bfloat16)


def draw_log_decay(key, part):
    lookup_segments = jax.random.split(jax.random.fold_in(key, 4), 7)
    record_entries = HEADS // 2
    spans = CONTEXT_LENGTH // TOK_DEV
    fast_share = 0.5
    quick = jax.random.uniform(lookup_segments[0], (record_entries,), jnp.float32) < fast_share
    quick_rate = jnp.exp(jax.random.uniform(lookup_segments[1], (record_entries,), jnp.float32, math.log(1.0 / 50.0), math.log(1.0 / 30.0)))
    slow_rate = jnp.exp(jax.random.uniform(lookup_segments[2], (record_entries,), jnp.float32, math.log(0.1), math.log(0.4))) / CONTEXT_LENGTH
    rate = jnp.where(quick, quick_rate, slow_rate)
    factor = jnp.exp(jax.random.uniform(lookup_segments[3], (spans, record_entries), jnp.float32, -0.7, 0.7))
    factor = jnp.repeat(factor, TOK_DEV, axis=0)
    rough = jax.random.uniform(lookup_segments[4], (CONTEXT_LENGTH, record_entries), jnp.float32, 0.5, 1.5)
    steady = -rate[None, :] * factor * rough
    segment_offset = jax.random.randint(lookup_segments[5], (3, record_entries), 0, CONTEXT_LENGTH)
    excluded_filter = jnp.any(jnp.arange(CONTEXT_LENGTH)[:, None, None] == segment_offset[None, :, :], axis=1)
    loss = jnp.log(jax.random.uniform(lookup_segments[6], (CONTEXT_LENGTH, record_entries), jnp.float32, 0.5, 0.8))
    return jnp.where(excluded_filter, loss, steady)


def draw_selection(key, part):
    count = CONTEXT_LENGTH // BLK
    own_key = jax.random.fold_in(key, 7013)
    columns = jnp.arange(count, dtype=jnp.int32)
    draws = jax.random.randint(own_key, (count, count), 0, 1048576, jnp.int32)
    scores = draws * count + columns[None, :]
    record_entries = columns[:, None]
    scores = jnp.where(columns[None, :] < record_entries, scores, -1 - columns[None, :])
    best_scores, best = lax.top_k(scores, 2)
    chosen = jnp.where(best_scores >= 0, best, record_entries)
    return jnp.concatenate([record_entries, chosen], axis=1).astype(jnp.int32)


def setup_inputs(seed: int = 0) -> dict:
    splits = jax.random.split(jax.random.key(seed), 7)
    queries = draw_queries(jax.random.fold_in(splits[6], 71), 0)
    keys = draw_keys(jax.random.fold_in(splits[6], 71), 0)
    values = draw_values(jax.random.fold_in(splits[6], 71), 0)
    log_decay = draw_log_decay(jax.random.fold_in(splits[6], 71), 0)
    selection = draw_selection(jax.random.fold_in(splits[6], 71), 0)
    out_gain = jnp.clip(1.0 + 0.1 * jax.random.normal(splits[5], (HEADS * HD,), jnp.float32), 0.5, 1.5)
    return dict(queries=queries, keys=keys, values=values, log_decay=log_decay, selection=selection, out_gain=out_gain)


EPSILON = 1e-06
NEGATIVE = -1e+30
HIGHEST = lax.Precision.HIGHEST

def within_spans(query_lin, key_lin, value_lin, log_decay, span):
    rows, record_entries, width = query_lin.shape
    count = rows // span
    probe_segments = query_lin.reshape(count, span, record_entries, width).astype(jnp.float32)
    key_spans = key_lin.reshape(count, span, record_entries, width).astype(jnp.float32)
    value_spans = value_lin.reshape(count, span, record_entries, width).astype(jnp.float32)
    running = jnp.cumsum(log_decay.reshape(count, span, record_entries), axis=1)
    by_line = jnp.transpose(running, (0, 2, 1))
    causal = jnp.arange(span)[:, None] >= jnp.arange(span)[None, :]
    stride_gap = jnp.where(causal, by_line[:, :, :, None] - by_line[:, :, None, :], 0.0)
    damping = jnp.where(causal, jnp.exp(stride_gap), 0.0)
    scores = jnp.einsum('ctld,csld->clts', probe_segments, key_spans)
    mixing = (scores * damping).astype(jnp.bfloat16)
    inside = jnp.einsum('clts,csld->ctld', mixing.astype(jnp.float32), value_spans)
    ending = running[:, -1, :]
    weighted_keys = (key_spans * jnp.exp(ending[:, None, :] - running)[..., None]).astype(jnp.bfloat16)
    increments = jnp.einsum('ctld,ctle->clde', weighted_keys.astype(jnp.float32), value_spans)

    def advance(state, inputs):
        decay_sum, increment = inputs
        return (jnp.exp(decay_sum)[:, None, None] * state + increment, state)
    final_state, entering = lax.scan(advance, jnp.zeros((record_entries, width, width), jnp.float32), (ending, increments))
    weighted_queries = probe_segments * jnp.exp(running)[..., None]
    across = jnp.einsum('ctld,clde->ctle', weighted_queries, entering, precision=HIGHEST)
    return (inside + across).reshape(rows, record_entries, width)

def attend_tiles(query, key_tiles, payload_blocks, query_pos, slot_open, per_slot):
    rows, record_entries, width = query.shape
    tile_len = key_tiles.shape[1]
    scale = width ** (-0.5)
    query_wide = query.astype(jnp.float32)

    def tile_step(tile, carry):
        best, total, accum = carry
        slot = tile // per_slot
        key_pos = tile % per_slot * tile_len + jnp.arange(tile_len)
        key_tile = lax.dynamic_index_in_dim(key_tiles, tile, 0, keepdims=False).astype(jnp.float32)
        value_tile = lax.dynamic_index_in_dim(payload_blocks, tile, 0, keepdims=False).astype(jnp.float32)
        causal = key_pos[None, :] <= query_pos[:, None]
        allowed = jnp.where(slot == 0, causal, slot_open[slot])
        scores = jnp.einsum('ild,jld->lij', query_wide, key_tile) * scale
        masked = jnp.where(allowed[None], scores, NEGATIVE)
        tile_max = lax.optimization_barrier(jnp.max(masked, axis=2))
        probs = jnp.where(allowed[None], jnp.exp(masked - tile_max[:, :, None]), 0.0).astype(jnp.bfloat16)
        tile_sum = lax.optimization_barrier(jnp.sum(probs, axis=2, dtype=jnp.float32))
        tile_out = jnp.einsum('lij,jld->ild', probs.astype(jnp.float32), value_tile)
        peak = jnp.maximum(best, tile_max)
        keep = jnp.exp(best - peak)
        fresh = jnp.exp(tile_max - peak)
        total = total * keep + tile_sum * fresh
        accum = accum * keep.T[:, :, None] + tile_out * fresh.T[:, :, None]
        return (peak, total, accum)
    start = (jnp.full((record_entries, rows), NEGATIVE, jnp.float32), jnp.zeros((record_entries, rows), jnp.float32), jnp.zeros((rows, record_entries, width), jnp.float32))
    best, total, accum = lax.fori_loop(0, key_tiles.shape[0], tile_step, start)
    return accum / total.T[:, :, None]

def block_attention(query_heads, key_heads, value_heads, selection):
    count = CONTEXT_LENGTH // BLK
    per_slot = BLK // TILE
    record_entries = query_heads.shape[1]
    query_blocks = query_heads.reshape(count, BLK, record_entries, HD)
    key_blocks = key_heads.reshape(count, BLK, record_entries, HD)
    value_blocks = value_heads.reshape(count, BLK, record_entries, HD)

    def one_block(index):
        query = lax.dynamic_index_in_dim(query_blocks, index, 0, keepdims=False)
        chosen = lax.dynamic_index_in_dim(selection, index, 0, keepdims=False).astype(jnp.int32)
        key_here = jnp.take(key_blocks, chosen, axis=0).reshape(3 * per_slot, TILE, record_entries, HD)
        value_here = jnp.take(value_blocks, chosen, axis=0).reshape(3 * per_slot, TILE, record_entries, HD)
        slot_open = jnp.concatenate([jnp.ones((1,), jnp.bool_), chosen[1:] != index])
        return attend_tiles(query, key_here, value_here, jnp.arange(BLK), slot_open, per_slot)
    result = lax.map(one_block, jnp.arange(count, dtype=jnp.int32))
    return result.reshape(CONTEXT_LENGTH, record_entries, HD)

def normalize(heads):
    return heads * lax.rsqrt(lax.optimization_barrier(jnp.mean(heads * heads, axis=-1, keepdims=True)) + EPSILON)

def reference(queries, keys, values, log_decay, selection, out_gain):
    pairs = HEADS // 2
    query_pairs = queries.reshape(CONTEXT_LENGTH, pairs, 2, HD)
    paired_keys = keys.reshape(CONTEXT_LENGTH, pairs, 2, HD)
    paired_values = values.reshape(CONTEXT_LENGTH, pairs, 2, HD)
    linear = within_spans(query_pairs[:, :, 0], paired_keys[:, :, 0], paired_values[:, :, 0], log_decay, CH)
    attended = block_attention(query_pairs[:, :, 1], paired_keys[:, :, 1], paired_values[:, :, 1], selection)
    both = jnp.stack([normalize(linear), normalize(attended)], axis=2).reshape(CONTEXT_LENGTH, HEADS * HD)
    return (both * out_gain[None, :]).astype(jnp.bfloat16)
```

```python
import jax
import jax.numpy as jnp
from jax import lax
from jax.experimental import pallas as pl
from jax.experimental.pallas import tpu as pltpu
from jax.sharding import PartitionSpec as P

HD = 128
BLK = 4096
TILE = 1024
CH = 128


EPSILON = 1e-06
NEGATIVE = -1e30
HIGHEST = lax.Precision.HIGHEST
VMEM_LIMIT = 48 << 20
QROWS = 512


def carried_in(part, axis, combine, identity):
    place = lax.axis_index(axis)
    gathered = jax.tree.map(lambda a: lax.all_gather(a, axis), part)
    state = jax.tree.map(lambda a, e: jnp.zeros_like(a) + jnp.asarray(e, a.dtype), part, identity)

    def one(turn, state):
        return combine(
            state, jax.tree.map(lambda a: lax.dynamic_index_in_dim(a, turn, 0, False), gathered)
        )

    return lax.fori_loop(0, place, one, state)


def within_spans(query_lin, key_lin, value_lin, log_decay, span):
    rows, record_entries, width = query_lin.shape
    count = rows // span
    probe_segments = query_lin.reshape(count, span, record_entries, width)
    key_spans = key_lin.reshape(count, span, record_entries, width)
    value_spans = value_lin.reshape(count, span, record_entries, width)
    running = jnp.cumsum(log_decay.reshape(count, span, record_entries), axis=1)
    by_line = jnp.transpose(running, (0, 2, 1))
    causal = jnp.arange(span)[:, None] >= jnp.arange(span)[None, :]
    stride_gap = jnp.where(causal, by_line[:, :, :, None] - by_line[:, :, None, :], 0.0)
    damping = jnp.where(causal, jnp.exp(stride_gap), 0.0)
    scores = jnp.einsum(
        "ctld,csld->clts", probe_segments, key_spans, preferred_element_type=jnp.float32
    )
    mixing = (scores * damping).astype(jnp.bfloat16)
    inside = jnp.einsum("clts,csld->ctld", mixing, value_spans, preferred_element_type=jnp.float32)
    ending = running[:, -1, :]
    weighted_keys = (
        key_spans.astype(jnp.float32) * jnp.exp(ending[:, None, :] - running)[..., None]
    ).astype(jnp.bfloat16)
    increments = jnp.einsum(
        "ctld,ctle->clde", weighted_keys, value_spans, preferred_element_type=jnp.float32
    )

    def advance(state, inputs):
        decay_sum, increment = inputs
        return (jnp.exp(decay_sum)[:, None, None] * state + increment, state)

    final_state, entering = lax.scan(
        advance, jnp.zeros((record_entries, width, width), jnp.float32), (ending, increments)
    )
    weighted_queries = probe_segments.astype(jnp.float32) * jnp.exp(running)[..., None]
    across = jnp.einsum("ctld,clde->ctle", weighted_queries, entering, precision=HIGHEST)
    return (inside + across, weighted_queries, ending, final_state)


def attend_tiles(query, key_tiles, payload_blocks, query_pos, slot_open, per_slot):
    rows, record_entries, width = query.shape
    tile_len = key_tiles.shape[1]
    scale = width ** (-0.5)

    def tile_step(tile, carry):
        best, total, accum = carry
        slot = tile // per_slot
        key_pos = tile % per_slot * tile_len + jnp.arange(tile_len)
        key_tile = lax.dynamic_index_in_dim(key_tiles, tile, 0, keepdims=False)
        value_tile = lax.dynamic_index_in_dim(payload_blocks, tile, 0, keepdims=False)
        causal = key_pos[None, :] <= query_pos[:, None]
        allowed = jnp.where(slot == 0, causal, slot_open[slot])
        scores = (
            jnp.einsum("ild,jld->lij", query, key_tile, preferred_element_type=jnp.float32) * scale
        )
        masked = jnp.where(allowed[None], scores, NEGATIVE)
        tile_max = jnp.max(masked, axis=2)
        probs = jnp.where(allowed[None], jnp.exp(masked - tile_max[:, :, None]), 0.0).astype(
            jnp.bfloat16
        )
        tile_sum = jnp.sum(probs, axis=2, dtype=jnp.float32)
        tile_out = jnp.einsum("lij,jld->ild", probs, value_tile, preferred_element_type=jnp.float32)
        peak = jnp.maximum(best, tile_max)
        keep = jnp.exp(best - peak)
        fresh = jnp.exp(tile_max - peak)
        total = total * keep + tile_sum * fresh
        accum = accum * keep.T[:, :, None] + tile_out * fresh.T[:, :, None]
        return (peak, total, accum)

    start = (
        jnp.full((record_entries, rows), NEGATIVE, jnp.float32),
        jnp.zeros((record_entries, rows), jnp.float32),
        jnp.zeros((rows, record_entries, width), jnp.float32),
    )
    best, total, accum = lax.fori_loop(0, key_tiles.shape[0], tile_step, start)
    return accum / total.T[:, :, None]


def request_table(selection, group, seq_count):
    dest_block = jnp.arange(seq_count) // group
    chosen = jnp.take(selection, dest_block, axis=0)
    return jnp.transpose(chosen)[:, None, :] * group + jnp.arange(group)[None, :, None]


def normalize(heads):
    return heads * lax.rsqrt(jnp.mean(heads * heads, axis=-1, keepdims=True) + EPSILON)


def per_device(queries, keys, values, log_decay, selection, out_gain):
    queries, keys, values = (
        lax.all_to_all(queries, "head", split_axis=1, concat_axis=0, tiled=True),
        lax.all_to_all(keys, "head", split_axis=1, concat_axis=0, tiled=True),
        lax.all_to_all(values, "head", split_axis=1, concat_axis=0, tiled=True),
    )
    rows = queries.shape[0]
    width = HD
    pairs = queries.shape[1] // (2 * width)
    query_pairs = queries.reshape(rows, pairs, 2, width)
    paired_keys = keys.reshape(rows, pairs, 2, width)
    paired_values = values.reshape(rows, pairs, 2, width)
    linear_part, weighted_queries, ending, final_state = within_spans(
        query_pairs[:, :, 0], paired_keys[:, :, 0], paired_values[:, :, 0], log_decay, CH
    )
    total_decay = jnp.sum(ending, axis=0)

    def chain(earlier, later):
        return (earlier[0] + later[0], jnp.exp(later[0])[:, None, None] * earlier[1] + later[1])

    leading_decay, carried = carried_in(
        (total_decay, final_state),
        "seq",
        chain,
        (jnp.zeros_like(total_decay), jnp.zeros_like(final_state)),
    )
    span_start = jnp.cumsum(ending, axis=0) - ending
    shifted = weighted_queries * jnp.exp(span_start)[:, None, :, None]
    correction = jnp.einsum("ctld,lde->ctle", shifted, carried, precision=HIGHEST)
    linear_out = (linear_part + correction).reshape(rows, pairs, width)
    seq_count = lax.axis_size("seq")
    position = lax.axis_index("seq")
    group = BLK // rows
    block_index = position // group
    rank = position % group
    piece_rows = rows // seq_count
    query_moba = query_pairs[:, :, 1]
    key_moba = paired_keys[:, :, 1]
    value_moba = paired_values[:, :, 1]
    spread_keys, spread_values = (
        lax.all_to_all(
            key_moba.reshape(seq_count, piece_rows, pairs, width),
            "seq",
            split_axis=0,
            concat_axis=0,
            tiled=True,
        ),
        lax.all_to_all(
            value_moba.reshape(seq_count, piece_rows, pairs, width),
            "seq",
            split_axis=0,
            concat_axis=0,
            tiled=True,
        ),
    )
    table = request_table(selection, group, seq_count)
    block_keys, block_values = (
        lax.all_to_all(
            jnp.take(spread_keys, table, axis=0), "seq", split_axis=2, concat_axis=2, tiled=True
        ),
        lax.all_to_all(
            jnp.take(spread_values, table, axis=0), "seq", split_axis=2, concat_axis=2, tiled=True
        ),
    )
    block_keys = block_keys.reshape(3, BLK, pairs, width)
    block_values = block_values.reshape(3, BLK, pairs, width)
    per_slot = BLK // TILE
    key_tiles = block_keys.reshape(3 * per_slot, TILE, pairs, width)
    payload_blocks = block_values.reshape(3 * per_slot, TILE, pairs, width)
    chosen = jnp.take(selection, block_index, axis=0)
    slot_open = jnp.concatenate([jnp.ones((1,), jnp.bool_), chosen[1:] != block_index])
    query_pos = rank * rows + jnp.arange(rows)
    attended = attend_tiles(query_moba, key_tiles, payload_blocks, query_pos, slot_open, per_slot)
    both = jnp.stack([normalize(linear_out), normalize(attended)], axis=2).reshape(
        rows, pairs * 2 * width
    )
    return (both * out_gain[None, :]).astype(jnp.bfloat16)


SUB = 4
LOG2E = 1.4426950408889634


def dot_t(a, b):
    return lax.dot_general(a, b, (((1,), (1,)), ((), ())), preferred_element_type=jnp.float32)


def with_ones(v):
    return jnp.concatenate([v, jnp.ones(v.shape, v.dtype)], axis=1)


def own_block_kernel(q_ref, a_ref, b_ref, acc_ref, top_ref):
    i = pl.program_id(0)
    q = q_ref[0]
    rows = q.shape[0]
    scale = HD ** (-0.5) * LOG2E

    def keys_of(p):
        return jnp.concatenate([a_ref[p, 0], b_ref[p, 0]], axis=0)

    def values_of(p):
        return with_ones(jnp.concatenate([a_ref[p, 1], b_ref[p, 1]], axis=0))

    s = dot_t(q, keys_of(i)) * scale
    r = lax.broadcasted_iota(jnp.int32, s.shape, 0)
    c = lax.broadcasted_iota(jnp.int32, s.shape, 1)
    s = jnp.where(c <= r, s, NEGATIVE)
    m = jnp.max(s, axis=1, keepdims=True)
    prob = jnp.exp2(s - m).astype(jnp.bfloat16)
    top_ref[...] = jnp.broadcast_to(m, (rows, HD))
    acc_ref[...] = jnp.dot(prob, values_of(i), preferred_element_type=jnp.float32)

    @pl.loop(0, i)
    def _(p):
        s = dot_t(q, keys_of(p)) * scale
        old = top_ref[...]
        m = jnp.maximum(old, jnp.max(s, axis=1, keepdims=True))
        prob = jnp.exp2(s - m[:, :1]).astype(jnp.bfloat16)
        keep = jnp.exp2(old - m)
        top_ref[...] = m
        acc_ref[...] = acc_ref[...] * jnp.concatenate([keep, keep], axis=1) + jnp.dot(
            prob, values_of(p), preferred_element_type=jnp.float32
        )


def own_block(q, part_a, part_b):
    sources, rows, width = q.shape
    tokens = sources * rows
    return pl.pallas_call(
        own_block_kernel,
        grid=(sources,),
        in_specs=[
            pl.BlockSpec((1, rows, width), lambda i: (i, 0, 0)),
            pl.BlockSpec(part_a.shape, lambda i: (0, 0, 0, 0)),
            pl.BlockSpec(part_b.shape, lambda i: (0, 0, 0, 0)),
        ],
        out_specs=[
            pl.BlockSpec((rows, 2 * width), lambda i: (i, 0)),
            pl.BlockSpec((rows, width), lambda i: (i, 0)),
        ],
        out_shape=[
            jax.ShapeDtypeStruct((tokens, 2 * width), jnp.float32),
            jax.ShapeDtypeStruct((tokens, width), jnp.float32),
        ],
        compiler_params=pltpu.CompilerParams(vmem_limit_bytes=VMEM_LIMIT),
        cost_estimate=pl.CostEstimate(
            flops=4 * tokens * tokens * width // 2, bytes_accessed=12 << 20, transcendentals=tokens * tokens // 2
        ),
        name="own_block",
    )(q, part_a, part_b)


def fold_chunk(q, kv_ref, count, acc, old):
    scale = HD ** (-0.5) * LOG2E
    sources, _, rows, width = kv_ref.shape
    k = kv_ref[:, 0].reshape(sources * rows, width)
    v = kv_ref[:, 1].reshape(sources * rows, width)
    s = dot_t(q, k) * scale
    m = jnp.maximum(old, jnp.max(s, axis=1, keepdims=True))
    prob = jnp.exp2(s - m[:, :1]).astype(jnp.bfloat16)
    keep = jnp.exp2(old - m)
    acc = acc * jnp.concatenate([keep, keep], axis=1) + count * jnp.dot(
        prob, with_ones(v), preferred_element_type=jnp.float32
    )
    return acc, m


def chunk_kernel(meta_ref, q_ref, kv_ref, acc_in, top_in, acc_out, top_out):
    count = meta_ref[0]

    @pl.when(count > 0)
    def _():
        acc_out[...], top_out[...] = fold_chunk(
            q_ref[...], kv_ref, count.astype(jnp.float32), acc_in[...], top_in[...]
        )

    @pl.when(count == 0)
    def _():
        acc_out[...] = acc_in[...]
        top_out[...] = top_in[...]


def chunk_cost(tokens, keys, width):
    return pl.CostEstimate(
        flops=4 * tokens * keys * width, bytes_accessed=12 << 20, transcendentals=tokens * keys
    )


def fold(meta, q, kv, acc, top, rows=QROWS):
    tokens, width = q.shape
    keys = kv.shape[0] * kv.shape[2]
    return pl.pallas_call(
        chunk_kernel,
        grid_spec=pltpu.PrefetchScalarGridSpec(
            num_scalar_prefetch=1,
            grid=(tokens // rows,),
            in_specs=[
                pl.BlockSpec((rows, width), lambda i, s: (i, 0)),
                pl.BlockSpec(kv.shape, lambda i, s: (0, 0, 0, 0)),
                pl.BlockSpec((rows, 2 * width), lambda i, s: (i, 0)),
                pl.BlockSpec((rows, width), lambda i, s: (i, 0)),
            ],
            out_specs=[
                pl.BlockSpec((rows, 2 * width), lambda i, s: (i, 0)),
                pl.BlockSpec((rows, width), lambda i, s: (i, 0)),
            ],
        ),
        out_shape=[
            jax.ShapeDtypeStruct(acc.shape, jnp.float32),
            jax.ShapeDtypeStruct(top.shape, jnp.float32),
        ],
        input_output_aliases={3: 0, 4: 1},
        compiler_params=pltpu.CompilerParams(vmem_limit_bytes=VMEM_LIMIT),
        cost_estimate=chunk_cost(tokens, keys, width),
        name="fold_chunk",
    )(meta, q, kv, acc, top)


def last_kernel(meta_ref, q_ref, kv_ref, acc_in, top_in, gain_ref, out_ref):
    count = meta_ref[0]

    def finish(acc):
        out = acc[:, :HD] / acc[:, HD:]
        out_ref[...] = (normalize(out) * gain_ref[...]).astype(jnp.bfloat16)

    @pl.when(count > 0)
    def _():
        acc, _ = fold_chunk(q_ref[...], kv_ref, count.astype(jnp.float32), acc_in[...], top_in[...])
        finish(acc)

    @pl.when(count == 0)
    def _():
        finish(acc_in[...])


def fold_last(meta, q, kv, acc, top, gain, rows=QROWS):
    tokens, width = q.shape
    keys = kv.shape[0] * kv.shape[2]
    steps = tokens // rows // 2
    return pl.pallas_call(
        last_kernel,
        grid_spec=pltpu.PrefetchScalarGridSpec(
            num_scalar_prefetch=1,
            grid=(steps,),
            in_specs=[
                pl.BlockSpec((rows, width), lambda i, s: (s[1] * steps + i, 0)),
                pl.BlockSpec(kv.shape, lambda i, s: (0, 0, 0, 0)),
                pl.BlockSpec((rows, 2 * width), lambda i, s: (s[1] * steps + i, 0)),
                pl.BlockSpec((rows, width), lambda i, s: (s[1] * steps + i, 0)),
                pl.BlockSpec((1, width), lambda i, s: (0, 0)),
            ],
            out_specs=pl.BlockSpec((rows, width), lambda i, s: (i, 0)),
        ),
        out_shape=jax.ShapeDtypeStruct((tokens // 2, width), jnp.bfloat16),
        compiler_params=pltpu.CompilerParams(vmem_limit_bytes=VMEM_LIMIT),
        cost_estimate=chunk_cost(tokens // 2, keys, width),
        name="fold_last",
    )(meta, q, kv, acc, top, gain)


def states_kernel(kv_ref, weight_ref, decay_ref, entering_ref, final_ref):
    spans = entering_ref.shape[0]
    state = jnp.zeros((HD, HD), jnp.float32)
    for s in range(spans):
        rows = pl.ds(s % SUB * CH, CH)
        entering_ref[s] = state
        k = kv_ref[s // SUB, 0, rows, :].astype(jnp.float32)
        v = kv_ref[s // SUB, 1, rows, :]
        weighted = (k * weight_ref[:, s : s + 1]).astype(jnp.bfloat16)
        inc = lax.dot_general(
            weighted, v, (((0,), (0,)), ((), ())), preferred_element_type=jnp.float32
        )
        state = decay_ref[s : s + 1, :] * state + inc
    final_ref[...] = state


def states(kv, weight, decay):
    spans = decay.shape[0]
    return pl.pallas_call(
        states_kernel,
        out_shape=[
            jax.ShapeDtypeStruct((spans, HD, HD), jnp.float32),
            jax.ShapeDtypeStruct((HD, HD), jnp.float32),
        ],
        compiler_params=pltpu.CompilerParams(vmem_limit_bytes=VMEM_LIMIT),
        cost_estimate=pl.CostEstimate(flops=2 * spans * CH * HD * HD * 4, bytes_accessed=4 << 20, transcendentals=0),
        name="span_states",
    )(kv, weight, decay)


def linear_kernel(q_ref, kv_ref, entering_ref, carried_ref, cum_ref, cum_t_ref, lead_ref, gain_ref, out_ref):
    spans = entering_ref.shape[0]
    r = lax.broadcasted_iota(jnp.int32, (CH, CH), 0)
    c = lax.broadcasted_iota(jnp.int32, (CH, CH), 1)
    causal = c <= r
    for s in range(spans):
        rows = pl.ds(s % SUB * CH, CH)
        q = q_ref[s // SUB, rows, :]
        k = kv_ref[s // SUB, 0, rows, :]
        v = kv_ref[s // SUB, 1, rows, :]
        column = cum_t_ref[:, s : s + 1]
        gap = jnp.where(causal, column - cum_ref[s : s + 1, :], 0.0)
        damping = jnp.where(causal, jnp.exp(gap), 0.0)
        mixing = (dot_t(q, k) * damping).astype(jnp.bfloat16)
        inside = jnp.dot(mixing, v, preferred_element_type=jnp.float32)
        state = entering_ref[s] + lead_ref[s : s + 1, :] * carried_ref[...]
        high = state.astype(jnp.bfloat16)
        low = (state - high.astype(jnp.float32)).astype(jnp.bfloat16)
        across = jnp.dot(q, jnp.concatenate([high, low], axis=1), preferred_element_type=jnp.float32)
        out = inside + jnp.exp(column) * (across[:, :HD] + across[:, HD:])
        out_ref[s * CH : (s + 1) * CH, :] = (normalize(out) * gain_ref[...]).astype(jnp.bfloat16)


def linear(q, kv, entering, carried, cum, cum_t, lead, gain):
    spans = cum.shape[0]
    return pl.pallas_call(
        linear_kernel,
        out_shape=jax.ShapeDtypeStruct((spans * CH, HD), jnp.bfloat16),
        compiler_params=pltpu.CompilerParams(vmem_limit_bytes=VMEM_LIMIT),
        cost_estimate=pl.CostEstimate(flops=2 * spans * CH * HD * HD * 6, bytes_accessed=6 << 20, transcendentals=0),
        name="linear_heads",
    )(q, kv, entering, carried, cum, cum_t, lead, gain)


def paired_device(queries, keys, values, log_decay, selection, out_gain):
    plane = ("x", "y", "c")
    z, x = lax.axis_index("z"), lax.axis_index("x")
    tokens = queries.shape[0]
    half = tokens // 2
    order = [4 * y + 2 * c + xx for xx in range(2) for y in range(2) for c in range(2)]

    def columns(a, kind, start, stop):
        return [a[start:stop, (2 * j + kind) * HD : (2 * j + kind + 1) * HD] for j in order]

    def to_heads(parts):
        return lax.all_to_all(parts, plane, 0, 0, tiled=True)

    def pair_up(kind, start, stop):
        return jnp.stack(
            [jnp.stack(t) for t in zip(columns(keys, kind, start, stop), columns(values, kind, start, stop))]
        )

    part_a = to_heads(pair_up(1, 0, half))
    part_b = to_heads(pair_up(1, half, tokens))
    q_att = to_heads(jnp.stack(columns(queries, 1, 0, tokens)))
    kv_lin = to_heads(pair_up(0, 0, tokens))
    q_lin = to_heads(jnp.stack(columns(queries, 0, 0, tokens)))

    others = selection[:, 1:]
    rows_of = jnp.arange(selection.shape[0])

    def count(i, b):
        return jnp.sum((others[i] == b) & (others[i] != i)).astype(jnp.int32)

    two, one = count(3, 2) > 0, count(3, 1) > 0
    both = two & one
    c10, c20, c21 = count(1, 0), count(2, 0), count(2, 1)
    c30, c31, c32 = count(3, 0), count(3, 1), count(3, 2)
    none = jnp.int32(0)
    uses = jnp.stack(
        [
            jnp.stack([none, none, none, none, none]),
            jnp.stack([c10, c10, none, none, none]),
            jnp.stack([c21, c21, c20, c20, none]),
            jnp.stack(
                [
                    c32,
                    jnp.where(two, c32, c31),
                    c31,
                    jnp.where(both, c31, c30),
                    jnp.where(both, none, c30),
                ]
            ),
        ]
    )
    mine = lax.dynamic_index_in_dim(uses, z, 0, False)

    sender = z == 2
    up = [(0, 1), (1, 2), (2, 3)]
    r1 = lax.ppermute(part_a, "z", up)
    r2 = lax.ppermute(jnp.where(sender & ~two, r1, part_b), "z", up)
    r3 = lax.ppermute(jnp.where(sender & ~two, r2, r1), "z", up[1:])
    r4 = lax.ppermute(jnp.where(sender & ~both, r3, r2), "z", up[1:])
    r5 = lax.ppermute(r4, "z", up[2:])

    gain = lax.dynamic_slice_in_dim(out_gain, x * 2 * HD, 2 * HD).reshape(2, 1, HD)
    acc, top = own_block(q_att, part_a, part_b)
    q_flat = q_att.reshape(-1, HD)
    for step, kv in enumerate((r1, r2, r3, r4)):
        acc, top = fold(mine[step : step + 1], q_flat, kv, acc, top)

    swap = [(0, 1), (1, 0)]
    own_decay = lax.dynamic_index_in_dim(log_decay, x, 1, False)
    sent_decay = lax.dynamic_index_in_dim(log_decay, 1 - x, 1, False)
    got_decay = lax.ppermute(sent_decay, "x", swap)
    decays = jnp.where(x == 0, jnp.stack([own_decay, got_decay]), jnp.stack([got_decay, own_decay]))
    cum = jnp.cumsum(decays.reshape(-1, CH), axis=1)
    ending = cum[:, -1]
    spans = cum.shape[0]
    weight = jnp.exp(ending[:, None] - cum).T
    decay = jnp.broadcast_to(jnp.exp(ending)[:, None], (spans, HD))
    lead = jnp.broadcast_to(jnp.exp(jnp.cumsum(ending) - ending)[:, None], (spans, HD))
    entering, final = states(kv_lin, weight, decay)
    whole = jnp.exp(jnp.sum(ending))
    carried = jnp.zeros_like(final)
    for _ in range(3):
        carried = lax.ppermute(whole * carried + final, "z", up)
    lin = linear(q_lin, kv_lin, entering, carried, cum, cum.T, lead, gain[0])
    rows = lin.shape[0] // 2
    lin_own = lax.dynamic_slice_in_dim(lin, x * rows, rows)
    lin_got = lax.ppermute(lax.dynamic_slice_in_dim(lin, (1 - x) * rows, rows), "x", swap)

    away = fold_last(jnp.stack([mine[4], 1 - x]), q_flat, r5, acc, top, gain[1])
    att_got = lax.ppermute(away, "x", swap)
    att_own = fold_last(jnp.stack([mine[4], x]), q_flat, r5, acc, top, gain[1])
    return jnp.where(
        x == 0,
        jnp.concatenate([lin_own, att_own, lin_got, att_got], axis=1),
        jnp.concatenate([lin_got, att_got, lin_own, att_own], axis=1),
    )


def solution(mesh):
    args = (P(("seq", "head"), None),) * 3 + (P("seq", "head"), P(), P("head"))
    if mesh.shape["seq"] == 8 and mesh.shape["head"] == 4:
        fine = jax.sharding.Mesh(mesh.devices.reshape(4, 2, 2, 2), ("z", "x", "y", "c"))
        everywhere = P(("z", "x", "y", "c"), None)
        return jax.shard_map(
            paired_device,
            mesh=fine,
            in_specs=(everywhere,) * 3 + (P(("z", "x"), ("y", "c")), P(), P(("y", "c"))),
            out_specs=P(("z", "x"), ("y", "c")),
            check_vma=False,
        )
    return jax.shard_map(
        per_device, mesh=mesh, in_specs=args, out_specs=P("seq", "head"), check_vma=False
    )
```

```python
import functools

import jax
import jax.numpy as jnp
from jax import lax
from jax.experimental import pallas as pl
from jax.experimental.pallas import tpu as pltpu
from jax.sharding import PartitionSpec as P

HD = 128
BLK = 4096
TILE = 1024
CH = 128


EPSILON = 1e-06
NEGATIVE = -1e30
HIGHEST = lax.Precision.HIGHEST
VMEM_LIMIT = 56 << 20


def carried_in(part, axis, combine, identity):
    place = lax.axis_index(axis)
    gathered = jax.tree.map(lambda a: lax.all_gather(a, axis), part)
    state = jax.tree.map(lambda a, e: jnp.zeros_like(a) + jnp.asarray(e, a.dtype), part, identity)

    def one(turn, state):
        return combine(
            state, jax.tree.map(lambda a: lax.dynamic_index_in_dim(a, turn, 0, False), gathered)
        )

    return lax.fori_loop(0, place, one, state)


def within_spans(query_lin, key_lin, value_lin, log_decay, span):
    rows, record_entries, width = query_lin.shape
    count = rows // span
    probe_segments = query_lin.reshape(count, span, record_entries, width)
    key_spans = key_lin.reshape(count, span, record_entries, width)
    value_spans = value_lin.reshape(count, span, record_entries, width)
    running = jnp.cumsum(log_decay.reshape(count, span, record_entries), axis=1)
    by_line = jnp.transpose(running, (0, 2, 1))
    causal = jnp.arange(span)[:, None] >= jnp.arange(span)[None, :]
    stride_gap = jnp.where(causal, by_line[:, :, :, None] - by_line[:, :, None, :], 0.0)
    damping = jnp.where(causal, jnp.exp(stride_gap), 0.0)
    scores = jnp.einsum(
        "ctld,csld->clts", probe_segments, key_spans, preferred_element_type=jnp.float32
    )
    mixing = (scores * damping).astype(jnp.bfloat16)
    inside = jnp.einsum("clts,csld->ctld", mixing, value_spans, preferred_element_type=jnp.float32)
    ending = running[:, -1, :]
    weighted_keys = (
        key_spans.astype(jnp.float32) * jnp.exp(ending[:, None, :] - running)[..., None]
    ).astype(jnp.bfloat16)
    increments = jnp.einsum(
        "ctld,ctle->clde", weighted_keys, value_spans, preferred_element_type=jnp.float32
    )

    def advance(state, inputs):
        decay_sum, increment = inputs
        return (jnp.exp(decay_sum)[:, None, None] * state + increment, state)

    final_state, entering = lax.scan(
        advance, jnp.zeros((record_entries, width, width), jnp.float32), (ending, increments)
    )
    weighted_queries = probe_segments.astype(jnp.float32) * jnp.exp(running)[..., None]
    across = jnp.einsum("ctld,clde->ctle", weighted_queries, entering, precision=HIGHEST)
    return (inside + across, weighted_queries, ending, final_state)


def attend_tiles(query, key_tiles, payload_blocks, query_pos, slot_open, per_slot):
    rows, record_entries, width = query.shape
    tile_len = key_tiles.shape[1]
    scale = width ** (-0.5)

    def tile_step(tile, carry):
        best, total, accum = carry
        slot = tile // per_slot
        key_pos = tile % per_slot * tile_len + jnp.arange(tile_len)
        key_tile = lax.dynamic_index_in_dim(key_tiles, tile, 0, keepdims=False)
        value_tile = lax.dynamic_index_in_dim(payload_blocks, tile, 0, keepdims=False)
        causal = key_pos[None, :] <= query_pos[:, None]
        allowed = jnp.where(slot == 0, causal, slot_open[slot])
        scores = (
            jnp.einsum("ild,jld->lij", query, key_tile, preferred_element_type=jnp.float32) * scale
        )
        masked = jnp.where(allowed[None], scores, NEGATIVE)
        tile_max = jnp.max(masked, axis=2)
        probs = jnp.where(allowed[None], jnp.exp(masked - tile_max[:, :, None]), 0.0).astype(
            jnp.bfloat16
        )
        tile_sum = jnp.sum(probs, axis=2, dtype=jnp.float32)
        tile_out = jnp.einsum("lij,jld->ild", probs, value_tile, preferred_element_type=jnp.float32)
        peak = jnp.maximum(best, tile_max)
        keep = jnp.exp(best - peak)
        fresh = jnp.exp(tile_max - peak)
        total = total * keep + tile_sum * fresh
        accum = accum * keep.T[:, :, None] + tile_out * fresh.T[:, :, None]
        return (peak, total, accum)

    start = (
        jnp.full((record_entries, rows), NEGATIVE, jnp.float32),
        jnp.zeros((record_entries, rows), jnp.float32),
        jnp.zeros((rows, record_entries, width), jnp.float32),
    )
    best, total, accum = lax.fori_loop(0, key_tiles.shape[0], tile_step, start)
    return accum / total.T[:, :, None]


def request_table(selection, group, seq_count):
    dest_block = jnp.arange(seq_count) // group
    chosen = jnp.take(selection, dest_block, axis=0)
    return jnp.transpose(chosen)[:, None, :] * group + jnp.arange(group)[None, :, None]


def normalize(heads):
    return heads * lax.rsqrt(jnp.mean(heads * heads, axis=-1, keepdims=True) + EPSILON)


def per_device(queries, keys, values, log_decay, selection, out_gain):
    queries, keys, values = (
        lax.all_to_all(queries, "head", split_axis=1, concat_axis=0, tiled=True),
        lax.all_to_all(keys, "head", split_axis=1, concat_axis=0, tiled=True),
        lax.all_to_all(values, "head", split_axis=1, concat_axis=0, tiled=True),
    )
    rows = queries.shape[0]
    width = HD
    pairs = queries.shape[1] // (2 * width)
    query_pairs = queries.reshape(rows, pairs, 2, width)
    paired_keys = keys.reshape(rows, pairs, 2, width)
    paired_values = values.reshape(rows, pairs, 2, width)
    linear_part, weighted_queries, ending, final_state = within_spans(
        query_pairs[:, :, 0], paired_keys[:, :, 0], paired_values[:, :, 0], log_decay, CH
    )
    total_decay = jnp.sum(ending, axis=0)

    def chain(earlier, later):
        return (earlier[0] + later[0], jnp.exp(later[0])[:, None, None] * earlier[1] + later[1])

    leading_decay, carried = carried_in(
        (total_decay, final_state),
        "seq",
        chain,
        (jnp.zeros_like(total_decay), jnp.zeros_like(final_state)),
    )
    span_start = jnp.cumsum(ending, axis=0) - ending
    shifted = weighted_queries * jnp.exp(span_start)[:, None, :, None]
    correction = jnp.einsum("ctld,lde->ctle", shifted, carried, precision=HIGHEST)
    linear_out = (linear_part + correction).reshape(rows, pairs, width)
    seq_count = lax.axis_size("seq")
    position = lax.axis_index("seq")
    group = BLK // rows
    block_index = position // group
    rank = position % group
    piece_rows = rows // seq_count
    query_moba = query_pairs[:, :, 1]
    key_moba = paired_keys[:, :, 1]
    value_moba = paired_values[:, :, 1]
    spread_keys, spread_values = (
        lax.all_to_all(
            key_moba.reshape(seq_count, piece_rows, pairs, width),
            "seq",
            split_axis=0,
            concat_axis=0,
            tiled=True,
        ),
        lax.all_to_all(
            value_moba.reshape(seq_count, piece_rows, pairs, width),
            "seq",
            split_axis=0,
            concat_axis=0,
            tiled=True,
        ),
    )
    table = request_table(selection, group, seq_count)
    block_keys, block_values = (
        lax.all_to_all(
            jnp.take(spread_keys, table, axis=0), "seq", split_axis=2, concat_axis=2, tiled=True
        ),
        lax.all_to_all(
            jnp.take(spread_values, table, axis=0), "seq", split_axis=2, concat_axis=2, tiled=True
        ),
    )
    block_keys = block_keys.reshape(3, BLK, pairs, width)
    block_values = block_values.reshape(3, BLK, pairs, width)
    per_slot = BLK // TILE
    key_tiles = block_keys.reshape(3 * per_slot, TILE, pairs, width)
    payload_blocks = block_values.reshape(3 * per_slot, TILE, pairs, width)
    chosen = jnp.take(selection, block_index, axis=0)
    slot_open = jnp.concatenate([jnp.ones((1,), jnp.bool_), chosen[1:] != block_index])
    query_pos = rank * rows + jnp.arange(rows)
    attended = attend_tiles(query_moba, key_tiles, payload_blocks, query_pos, slot_open, per_slot)
    both = jnp.stack([normalize(linear_out), normalize(attended)], axis=2).reshape(
        rows, pairs * 2 * width
    )
    return (both * out_gain[None, :]).astype(jnp.bfloat16)


SUB = 4
QUARTER = 128
SUMS = 16
QT = 1024
LOG2E = 1.4426950408889634


def dot_t(a, b):
    return lax.dot_general(a, b, (((1,), (1,)), ((), ())), preferred_element_type=jnp.float32)


def scaled(q):
    wide = q.astype(jnp.float32) * (HD ** (-0.5) * LOG2E)
    high = wide.astype(jnp.bfloat16)
    return jnp.concatenate([high, (wide - high.astype(jnp.float32)).astype(jnp.bfloat16)], axis=1)


def place(k, v, k_ref, v_ref, at):
    rows = k.shape[0]
    k_ref[at : at + rows, :] = jnp.concatenate([k, k], axis=1)
    v_ref[:HD, at : at + rows] = v.T
    v_ref[HD:, at : at + rows] = jnp.ones((SUMS, rows), jnp.bfloat16)


def estimate(us, transcendentals=0):
    return pl.CostEstimate(flops=int(us * 1.1e9), bytes_accessed=1 << 20, transcendentals=transcendentals)


def params(limit=VMEM_LIMIT):
    return pltpu.CompilerParams(vmem_limit_bytes=limit)


def first_pack_kernel(k_ref, v_ref, out_ref):
    out_ref[0, 0] = k_ref[...]
    out_ref[0, 1] = v_ref[...]


def taker(p):
    return 2 * (p % 4) + p // 4


def first_pack(keys, values):
    tokens = keys.shape[0]
    spec = pl.BlockSpec((tokens // 2, HD), lambda p: (0, 2 * taker(p) + 1))
    return pl.pallas_call(
        first_pack_kernel,
        grid=(8,),
        in_specs=[spec, spec],
        out_specs=pl.BlockSpec((1, 2, tokens // 2, HD), lambda p: (p, 0, 0, 0)),
        out_shape=jax.ShapeDtypeStruct((8, 2, tokens // 2, HD), jnp.bfloat16),
        compiler_params=params(),
        cost_estimate=estimate(2),
        name="pack_first_keys",
    )(keys, values)


def pack_kernel(q_ref, k_ref, v_ref, b_ref, q_out, lin_ref):
    half = b_ref.shape[2]
    b_ref[0, 0] = k_ref[half:, HD:]
    b_ref[0, 1] = v_ref[half:, HD:]
    q_out[0] = q_ref[:, HD:]
    lin_ref[0, 0] = q_ref[:, :HD]
    lin_ref[0, 1] = k_ref[:, :HD]
    lin_ref[0, 2] = v_ref[:, :HD]


def pack(queries, keys, values):
    tokens = keys.shape[0]
    spec = pl.BlockSpec((tokens, 2 * HD), lambda p: (0, taker(p)))
    shapes = [(8, 2, tokens // 2, HD), (8, tokens, HD), (8, 3, tokens, HD)]
    return pl.pallas_call(
        pack_kernel,
        grid=(8,),
        in_specs=[spec, spec, spec],
        out_specs=[
            pl.BlockSpec((1,) + shape[1:], lambda p, n=len(shape): (p,) + (0,) * (n - 1))
            for shape in shapes
        ],
        out_shape=[jax.ShapeDtypeStruct(shape, jnp.bfloat16) for shape in shapes],
        compiler_params=params(),
        cost_estimate=estimate(5),
        name="pack_rest",
    )(queries, keys, values)


def own_kernel(away, pos_ref, q_ref, a_ref, b_ref, acc_ref, top_ref, k_ref, v_ref):
    tile = 2 * half_of(pos_ref, away) + pl.program_id(0)

    @pl.when(pl.program_id(0) == 0)
    def _():
        rows = a_ref.shape[2]
        for p in range(a_ref.shape[0]):
            for n, ref in enumerate((a_ref, b_ref)):
                place(ref[p, 0], ref[p, 1], k_ref, v_ref, (2 * p + n) * rows)

    q = scaled(q_ref[...].reshape(QT, HD))
    start = pl.multiple_of(tile * QT, QT)
    s = dot_t(k_ref[pl.ds(start, QT), :], q)
    key = lax.broadcasted_iota(jnp.int32, s.shape, 0)
    query = lax.broadcasted_iota(jnp.int32, s.shape, 1)
    s = jnp.where(key <= query, s, NEGATIVE)
    m = jnp.max(s, axis=0, keepdims=True)
    prob = jnp.exp2(s - m).astype(jnp.bfloat16)
    top_ref[...] = jnp.broadcast_to(m, top_ref.shape)
    acc_ref[...] = jnp.dot(v_ref[:, pl.ds(start, QT)], prob, preferred_element_type=jnp.float32)

    @pl.loop(0, tile)
    def _(p):
        begin = pl.multiple_of(p * QT, QT)
        s = dot_t(k_ref[pl.ds(begin, QT), :], q)
        old = top_ref[:1, :]
        m = jnp.maximum(old, jnp.max(s, axis=0, keepdims=True))
        prob = jnp.exp2(s - m).astype(jnp.bfloat16)
        top_ref[...] = jnp.broadcast_to(m, top_ref.shape)
        acc_ref[...] = acc_ref[...] * jnp.exp2(old - m) + jnp.dot(
            v_ref[:, pl.ds(begin, QT)], prob, preferred_element_type=jnp.float32
        )


def half_of(pos_ref, away):
    return 1 - pos_ref[1] if away else pos_ref[1]


def own_block(away, pos, q, part_a, part_b):
    sources, rows, width = q.shape
    tokens = sources * rows
    half = tokens // 2
    return pl.pallas_call(
        functools.partial(own_kernel, away),
        grid_spec=pltpu.PrefetchScalarGridSpec(
            num_scalar_prefetch=1,
            grid=(half // QT,),
            in_specs=[
                pl.BlockSpec((QT // rows, rows, width), lambda i, pos: (2 * half_of(pos, away) + i, 0, 0)),
                pl.BlockSpec(part_a.shape, lambda i, pos: (0, 0, 0, 0)),
                pl.BlockSpec(part_b.shape, lambda i, pos: (0, 0, 0, 0)),
            ],
            out_specs=[
                pl.BlockSpec((width + SUMS, QT), lambda i, pos: (0, i)),
                pl.BlockSpec((8, QT), lambda i, pos: (0, i)),
            ],
            scratch_shapes=[
                pltpu.VMEM((tokens, 2 * width), jnp.bfloat16),
                pltpu.VMEM((width + SUMS, tokens), jnp.bfloat16),
            ],
        ),
        out_shape=[
            jax.ShapeDtypeStruct((width + SUMS, half), jnp.float32),
            jax.ShapeDtypeStruct((8, half), jnp.float32),
        ],
        compiler_params=params(),
        cost_estimate=estimate(10),
        name="own_block",
    )(pos, q, part_a, part_b)


def times_used(pair, sel_ref, pos_ref):
    z = pos_ref[0]
    two = (sel_ref[3, 1] == 2) | (sel_ref[3, 2] == 2)
    both = two & ((sel_ref[3, 1] == 1) | (sel_ref[3, 2] == 1))
    first = 0 if pair < 2 else -1
    second = (1, 1, 0, 0, -1)[pair]
    third = (2, jnp.where(two, 2, 1), 1, jnp.where(both, 1, 0), jnp.where(both, -1, 0))[pair]
    block = jnp.where(z == 1, first, jnp.where(z == 2, second, jnp.where(z == 3, third, -1)))
    return (sel_ref[z, 1] == block).astype(jnp.int32) + (sel_ref[z, 2] == block).astype(jnp.int32)


def fold_kernel(pair, last, sel_ref, pos_ref, q_ref, c_ref, d_ref, acc_in, top_in, *refs):
    count = times_used(pair, sel_ref, pos_ref)
    k_ref, v_ref = refs[-2:]

    def folded():
        sources, _, rows, width = c_ref.shape
        keys = sources * rows
        for n, ref in enumerate((c_ref, d_ref)):
            place(
                ref[:, 0].reshape(keys, width), ref[:, 1].reshape(keys, width), k_ref, v_ref, n * keys
            )
        old = top_in[:1, :]
        s = dot_t(k_ref[...], scaled(q_ref[...].reshape(-1, width)))
        m = jnp.maximum(old, jnp.max(s, axis=0, keepdims=True))
        prob = jnp.exp2(s - m).astype(jnp.bfloat16)
        acc = acc_in[...] * jnp.exp2(old - m) + count.astype(jnp.float32) * jnp.dot(
            v_ref[...], prob, preferred_element_type=jnp.float32
        )
        return acc, m

    if last:
        gain_ref, out_ref = refs[:2]

        def finish(acc):
            out = acc[:HD] / acc[HD : HD + 1]
            out = out * lax.rsqrt(jnp.mean(out * out, axis=0, keepdims=True) + EPSILON)
            out_ref[...] = (out.T * gain_ref[...]).astype(jnp.bfloat16)

        @pl.when(count > 0)
        def _():
            finish(folded()[0])

        @pl.when(count == 0)
        def _():
            finish(acc_in[...])
    else:
        acc_out, top_out = refs[:2]

        @pl.when(count > 0)
        def _():
            acc, m = folded()
            acc_out[...] = acc
            top_out[...] = jnp.broadcast_to(m, top_out.shape)

        @pl.when(count == 0)
        def _():
            acc_out[...] = acc_in[...]
            top_out[...] = top_in[...]


def fold(pair, away, selection, pos, q, one, two, acc, top, gain=None):
    last = gain is not None
    sources, rows, width = q.shape
    half = sources * rows // 2
    keys = 2 * one.shape[0] * one.shape[2]
    chunk = pl.BlockSpec(one.shape, lambda i, sel, pos: (0, 0, 0, 0))
    flat = lambda i, sel, pos: (0, 0)
    acc_spec, top_spec = pl.BlockSpec(acc.shape, flat), pl.BlockSpec(top.shape, flat)
    return pl.pallas_call(
        functools.partial(fold_kernel, pair, last),
        grid_spec=pltpu.PrefetchScalarGridSpec(
            num_scalar_prefetch=2,
            grid=(1,),
            in_specs=[
                pl.BlockSpec((sources // 2, rows, width), lambda i, sel, pos: (half_of(pos, away), 0, 0)),
                chunk,
                chunk,
                acc_spec,
                top_spec,
            ]
            + ([pl.BlockSpec((1, width), flat)] if last else []),
            out_specs=pl.BlockSpec((half, width), flat) if last else [acc_spec, top_spec],
            scratch_shapes=[
                pltpu.VMEM((keys, 2 * width), jnp.bfloat16),
                pltpu.VMEM((width + SUMS, keys), jnp.bfloat16),
            ],
        ),
        out_shape=jax.ShapeDtypeStruct((half, width), jnp.bfloat16)
        if last
        else [jax.ShapeDtypeStruct(acc.shape, acc.dtype), jax.ShapeDtypeStruct(top.shape, top.dtype)],
        compiler_params=params(),
        cost_estimate=estimate(7),
        name="fold_last" if last else "fold_chunks",
    )(selection, pos, q, one, two, acc, top, *([gain] if last else []))


def states_kernel(lin_ref, weight_ref, decay_ref, entering_ref, final_ref):
    spans = entering_ref.shape[0]
    state = jnp.zeros((HD, HD), jnp.float32)
    for s in range(spans):
        rows = pl.ds(s % SUB * CH, CH)
        entering_ref[s] = state
        k = lin_ref[s // SUB, 1, rows, :].astype(jnp.float32)
        v = lin_ref[s // SUB, 2, rows, :]
        weighted = (k * weight_ref[:, s : s + 1]).astype(jnp.bfloat16)
        inc = lax.dot_general(
            weighted, v, (((0,), (0,)), ((), ())), preferred_element_type=jnp.float32
        )
        state = decay_ref[s : s + 1, :] * state + inc
    final_ref[...] = state


def states(lin, weight, decay):
    spans = decay.shape[0]
    return pl.pallas_call(
        states_kernel,
        out_shape=[
            jax.ShapeDtypeStruct((spans, HD, HD), jnp.float32),
            jax.ShapeDtypeStruct((HD, HD), jnp.float32),
        ],
        compiler_params=params(),
        cost_estimate=estimate(2),
        name="span_states",
    )(lin, weight, decay)


def linear_kernel(lin_ref, entering_ref, carried_ref, cum_ref, cum_t_ref, lead_ref, gain_ref, out_ref):
    spans = entering_ref.shape[0]
    r = lax.broadcasted_iota(jnp.int32, (CH, CH), 0)
    c = lax.broadcasted_iota(jnp.int32, (CH, CH), 1)
    causal = c <= r
    for s in range(spans):
        rows = pl.ds(s % SUB * CH, CH)
        q, k, v = (lin_ref[s // SUB, n, rows, :] for n in range(3))
        column = cum_t_ref[:, s : s + 1]
        gap = jnp.where(causal, column - cum_ref[s : s + 1, :], 0.0)
        damping = jnp.where(causal, jnp.exp(gap), 0.0)
        mixing = (dot_t(q, k) * damping).astype(jnp.bfloat16)
        inside = jnp.dot(mixing, v, preferred_element_type=jnp.float32)
        state = entering_ref[s] + lead_ref[s : s + 1, :] * carried_ref[...]
        high = state.astype(jnp.bfloat16)
        low = (state - high.astype(jnp.float32)).astype(jnp.bfloat16)
        across = jnp.dot(q, jnp.concatenate([high, low], axis=1), preferred_element_type=jnp.float32)
        out = inside + jnp.exp(column) * (across[:, :HD] + across[:, HD:])
        out_ref[s * CH : (s + 1) * CH, :] = (normalize(out) * gain_ref[...]).astype(jnp.bfloat16)


def linear(lin, entering, carried, cum, cum_t, lead, gain):
    spans = cum.shape[0]
    return pl.pallas_call(
        linear_kernel,
        out_shape=jax.ShapeDtypeStruct((spans * CH, HD), jnp.bfloat16),
        compiler_params=params(),
        cost_estimate=estimate(5),
        name="linear_heads",
    )(lin, entering, carried, cum, cum_t, lead, gain)


def paired_device(queries, keys, values, log_decay, selection, out_gain):
    z, x = lax.axis_index("z"), lax.axis_index("x")
    pos = jnp.stack([z, x]).astype(jnp.int32)

    def to_heads(parts):
        return lax.all_to_all(parts, ("x", "y", "c"), 0, 0, tiled=True)

    part_a = to_heads(first_pack(keys, values))
    part_b, q_att, lin_in = pack(queries, keys, values)
    part_b, q_att, lin_in = to_heads(part_b), to_heads(q_att), to_heads(lin_in)

    two = (selection[3, 1] == 2) | (selection[3, 2] == 2)
    both = two & ((selection[3, 1] == 1) | (selection[3, 2] == 1))
    early, late = (z == 2) & ~two, (z == 2) & ~both
    up = [(0, 1), (1, 2), (2, 3)]
    own = [part[:, :, i * QUARTER : (i + 1) * QUARTER] for part in (part_a, part_b) for i in range(2)]
    got = []
    for t in range(10):
        if t < 2:
            send = own[t]
        elif t < 4:
            send = jnp.where(early, got[t - 2], own[t])
        elif t < 6:
            send = jnp.where(early, got[t - 2], got[t - 4])
        elif t < 8:
            send = jnp.where(late, got[t - 2], got[t - 4])
        else:
            send = got[t - 2]
        got.append(lax.ppermute(send, "z", up if t < 4 else up[1:] if t < 8 else up[2:]))

    gains = lax.dynamic_slice_in_dim(out_gain, x * 2 * HD, 2 * HD).reshape(2, 1, HD)
    sums = [own_block(away, pos, q_att, part_a, part_b) for away in (True, False)]
    for pair in range(4):
        sums = [
            fold(pair, away, selection, pos, q_att, got[2 * pair], got[2 * pair + 1], *sums[n])
            for n, away in enumerate((True, False))
        ]

    swap = [(0, 1), (1, 0)]
    own_decay = lax.dynamic_index_in_dim(log_decay, x, 1, False)
    sent_decay = lax.dynamic_index_in_dim(log_decay, 1 - x, 1, False)
    got_decay = lax.ppermute(sent_decay, "x", swap)
    decays = jnp.where(x == 0, jnp.stack([own_decay, got_decay]), jnp.stack([got_decay, own_decay]))
    cum = jnp.cumsum(decays.reshape(-1, CH), axis=1)
    ending = cum[:, -1]
    spans = cum.shape[0]
    weight = jnp.exp(ending[:, None] - cum).T
    decay = jnp.broadcast_to(jnp.exp(ending)[:, None], (spans, HD))
    lead = jnp.broadcast_to(jnp.exp(jnp.cumsum(ending) - ending)[:, None], (spans, HD))
    entering, final = states(lin_in, weight, decay)
    whole = jnp.exp(jnp.sum(ending))
    carried = jnp.zeros_like(final)
    for _ in range(3):
        carried = lax.ppermute(whole * carried + final, "z", up)
    lin = linear(lin_in, entering, carried, cum, cum.T, lead, gains[0])
    rows = lin.shape[0] // 2
    lin_own = lax.dynamic_slice_in_dim(lin, x * rows, rows)
    lin_got = lax.ppermute(lax.dynamic_slice_in_dim(lin, (1 - x) * rows, rows), "x", swap)

    att_away = fold(4, True, selection, pos, q_att, got[8], got[9], *sums[0], gains[1])
    att_got = lax.ppermute(att_away, "x", swap)
    att_own = fold(4, False, selection, pos, q_att, got[8], got[9], *sums[1], gains[1])
    return jnp.where(
        x == 0,
        jnp.concatenate([lin_own, att_own, lin_got, att_got], axis=1),
        jnp.concatenate([lin_got, att_got, lin_own, att_own], axis=1),
    )


def solution(mesh):
    args = (P(("seq", "head"), None),) * 3 + (P("seq", "head"), P(), P("head"))
    if mesh.shape["seq"] == 8 and mesh.shape["head"] == 4:
        fine = jax.sharding.Mesh(mesh.devices.reshape(4, 2, 2, 2), ("z", "x", "y", "c"))
        everywhere = P(("z", "x", "y", "c"), None)
        return jax.shard_map(
            paired_device,
            mesh=fine,
            in_specs=(everywhere,) * 3 + (P(("z", "x"), ("y", "c")), P(), P(("y", "c"))),
            out_specs=P(("z", "x"), ("y", "c")),
            check_vma=False,
        )
    return jax.shard_map(
        per_device, mesh=mesh, in_specs=args, out_specs=P("seq", "head"), check_vma=False
    )
```

```python
import functools

import jax
import jax.numpy as jnp
from jax import lax
from jax.experimental import pallas as pl
from jax.experimental.pallas import tpu as pltpu
from jax.sharding import PartitionSpec as P

HD = 128
BLK = 4096
TILE = 1024
CH = 128


EPSILON = 1e-06
NEGATIVE = -1e30
HIGHEST = lax.Precision.HIGHEST
VMEM_LIMIT = 56 << 20


def carried_in(part, axis, combine, identity):
    place = lax.axis_index(axis)
    gathered = jax.tree.map(lambda a: lax.all_gather(a, axis), part)
    state = jax.tree.map(lambda a, e: jnp.zeros_like(a) + jnp.asarray(e, a.dtype), part, identity)

    def one(turn, state):
        return combine(
            state, jax.tree.map(lambda a: lax.dynamic_index_in_dim(a, turn, 0, False), gathered)
        )

    return lax.fori_loop(0, place, one, state)


def within_spans(query_lin, key_lin, value_lin, log_decay, span):
    rows, record_entries, width = query_lin.shape
    count = rows // span
    probe_segments = query_lin.reshape(count, span, record_entries, width)
    key_spans = key_lin.reshape(count, span, record_entries, width)
    value_spans = value_lin.reshape(count, span, record_entries, width)
    running = jnp.cumsum(log_decay.reshape(count, span, record_entries), axis=1)
    by_line = jnp.transpose(running, (0, 2, 1))
    causal = jnp.arange(span)[:, None] >= jnp.arange(span)[None, :]
    stride_gap = jnp.where(causal, by_line[:, :, :, None] - by_line[:, :, None, :], 0.0)
    damping = jnp.where(causal, jnp.exp(stride_gap), 0.0)
    scores = jnp.einsum(
        "ctld,csld->clts", probe_segments, key_spans, preferred_element_type=jnp.float32
    )
    mixing = (scores * damping).astype(jnp.bfloat16)
    inside = jnp.einsum("clts,csld->ctld", mixing, value_spans, preferred_element_type=jnp.float32)
    ending = running[:, -1, :]
    weighted_keys = (
        key_spans.astype(jnp.float32) * jnp.exp(ending[:, None, :] - running)[..., None]
    ).astype(jnp.bfloat16)
    increments = jnp.einsum(
        "ctld,ctle->clde", weighted_keys, value_spans, preferred_element_type=jnp.float32
    )

    def advance(state, inputs):
        decay_sum, increment = inputs
        return (jnp.exp(decay_sum)[:, None, None] * state + increment, state)

    final_state, entering = lax.scan(
        advance, jnp.zeros((record_entries, width, width), jnp.float32), (ending, increments)
    )
    weighted_queries = probe_segments.astype(jnp.float32) * jnp.exp(running)[..., None]
    across = jnp.einsum("ctld,clde->ctle", weighted_queries, entering, precision=HIGHEST)
    return (inside + across, weighted_queries, ending, final_state)


def attend_tiles(query, key_tiles, payload_blocks, query_pos, slot_open, per_slot):
    rows, record_entries, width = query.shape
    tile_len = key_tiles.shape[1]
    scale = width ** (-0.5)

    def tile_step(tile, carry):
        best, total, accum = carry
        slot = tile // per_slot
        key_pos = tile % per_slot * tile_len + jnp.arange(tile_len)
        key_tile = lax.dynamic_index_in_dim(key_tiles, tile, 0, keepdims=False)
        value_tile = lax.dynamic_index_in_dim(payload_blocks, tile, 0, keepdims=False)
        causal = key_pos[None, :] <= query_pos[:, None]
        allowed = jnp.where(slot == 0, causal, slot_open[slot])
        scores = (
            jnp.einsum("ild,jld->lij", query, key_tile, preferred_element_type=jnp.float32) * scale
        )
        masked = jnp.where(allowed[None], scores, NEGATIVE)
        tile_max = jnp.max(masked, axis=2)
        probs = jnp.where(allowed[None], jnp.exp(masked - tile_max[:, :, None]), 0.0).astype(
            jnp.bfloat16
        )
        tile_sum = jnp.sum(probs, axis=2, dtype=jnp.float32)
        tile_out = jnp.einsum("lij,jld->ild", probs, value_tile, preferred_element_type=jnp.float32)
        peak = jnp.maximum(best, tile_max)
        keep = jnp.exp(best - peak)
        fresh = jnp.exp(tile_max - peak)
        total = total * keep + tile_sum * fresh
        accum = accum * keep.T[:, :, None] + tile_out * fresh.T[:, :, None]
        return (peak, total, accum)

    start = (
        jnp.full((record_entries, rows), NEGATIVE, jnp.float32),
        jnp.zeros((record_entries, rows), jnp.float32),
        jnp.zeros((rows, record_entries, width), jnp.float32),
    )
    best, total, accum = lax.fori_loop(0, key_tiles.shape[0], tile_step, start)
    return accum / total.T[:, :, None]


def request_table(selection, group, seq_count):
    dest_block = jnp.arange(seq_count) // group
    chosen = jnp.take(selection, dest_block, axis=0)
    return jnp.transpose(chosen)[:, None, :] * group + jnp.arange(group)[None, :, None]


def normalize(heads):
    return heads * lax.rsqrt(jnp.mean(heads * heads, axis=-1, keepdims=True) + EPSILON)


def per_device(queries, keys, values, log_decay, selection, out_gain):
    queries, keys, values = (
        lax.all_to_all(queries, "head", split_axis=1, concat_axis=0, tiled=True),
        lax.all_to_all(keys, "head", split_axis=1, concat_axis=0, tiled=True),
        lax.all_to_all(values, "head", split_axis=1, concat_axis=0, tiled=True),
    )
    rows = queries.shape[0]
    width = HD
    pairs = queries.shape[1] // (2 * width)
    query_pairs = queries.reshape(rows, pairs, 2, width)
    paired_keys = keys.reshape(rows, pairs, 2, width)
    paired_values = values.reshape(rows, pairs, 2, width)
    linear_part, weighted_queries, ending, final_state = within_spans(
        query_pairs[:, :, 0], paired_keys[:, :, 0], paired_values[:, :, 0], log_decay, CH
    )
    total_decay = jnp.sum(ending, axis=0)

    def chain(earlier, later):
        return (earlier[0] + later[0], jnp.exp(later[0])[:, None, None] * earlier[1] + later[1])

    leading_decay, carried = carried_in(
        (total_decay, final_state),
        "seq",
        chain,
        (jnp.zeros_like(total_decay), jnp.zeros_like(final_state)),
    )
    span_start = jnp.cumsum(ending, axis=0) - ending
    shifted = weighted_queries * jnp.exp(span_start)[:, None, :, None]
    correction = jnp.einsum("ctld,lde->ctle", shifted, carried, precision=HIGHEST)
    linear_out = (linear_part + correction).reshape(rows, pairs, width)
    seq_count = lax.axis_size("seq")
    position = lax.axis_index("seq")
    group = BLK // rows
    block_index = position // group
    rank = position % group
    piece_rows = rows // seq_count
    query_moba = query_pairs[:, :, 1]
    key_moba = paired_keys[:, :, 1]
    value_moba = paired_values[:, :, 1]
    spread_keys, spread_values = (
        lax.all_to_all(
            key_moba.reshape(seq_count, piece_rows, pairs, width),
            "seq",
            split_axis=0,
            concat_axis=0,
            tiled=True,
        ),
        lax.all_to_all(
            value_moba.reshape(seq_count, piece_rows, pairs, width),
            "seq",
            split_axis=0,
            concat_axis=0,
            tiled=True,
        ),
    )
    table = request_table(selection, group, seq_count)
    block_keys, block_values = (
        lax.all_to_all(
            jnp.take(spread_keys, table, axis=0), "seq", split_axis=2, concat_axis=2, tiled=True
        ),
        lax.all_to_all(
            jnp.take(spread_values, table, axis=0), "seq", split_axis=2, concat_axis=2, tiled=True
        ),
    )
    block_keys = block_keys.reshape(3, BLK, pairs, width)
    block_values = block_values.reshape(3, BLK, pairs, width)
    per_slot = BLK // TILE
    key_tiles = block_keys.reshape(3 * per_slot, TILE, pairs, width)
    payload_blocks = block_values.reshape(3 * per_slot, TILE, pairs, width)
    chosen = jnp.take(selection, block_index, axis=0)
    slot_open = jnp.concatenate([jnp.ones((1,), jnp.bool_), chosen[1:] != block_index])
    query_pos = rank * rows + jnp.arange(rows)
    attended = attend_tiles(query_moba, key_tiles, payload_blocks, query_pos, slot_open, per_slot)
    both = jnp.stack([normalize(linear_out), normalize(attended)], axis=2).reshape(
        rows, pairs * 2 * width
    )
    return (both * out_gain[None, :]).astype(jnp.bfloat16)


SUB = 4
QUARTER = 128
SUMS = 16
TOP = HD + SUMS
SPEED = 2e7
LOG2E = 1.4426950408889634


def dot_t(a, b):
    return lax.dot_general(a, b, (((1,), (1,)), ((), ())), preferred_element_type=jnp.float32)


def scaled(q):
    wide = q.astype(jnp.float32) * (HD ** (-0.5) * LOG2E)
    high = wide.astype(jnp.bfloat16)
    return jnp.concatenate([high, (wide - high.astype(jnp.float32)).astype(jnp.bfloat16)], axis=1)


def place(k, v, k_ref, v_ref, at):
    rows = k.shape[0]
    k_ref[at : at + rows, :] = jnp.concatenate([k, k], axis=1)
    for i in range(0, rows, QUARTER):
        v_ref[:HD, at + i : at + i + QUARTER] = v[i : i + QUARTER, :]
    v_ref[HD:, at : at + rows] = jnp.ones((SUMS, rows), jnp.bfloat16)


def quarters(v):
    return jnp.concatenate([v[i : i + QUARTER].T for i in range(0, v.shape[0], QUARTER)], axis=0)


def estimate(us, transcendentals=0):
    return pl.CostEstimate(flops=int(us * SPEED), bytes_accessed=1 << 20, transcendentals=transcendentals)


def params(limit=VMEM_LIMIT):
    return pltpu.CompilerParams(vmem_limit_bytes=limit)


def taker(p):
    return 2 * (p % 4) + p // 4


def first_pack_kernel(q_ref, k_ref, v_ref, out_ref):
    rows = k_ref.shape[0]
    for p in range(8):
        at = pl.ds((2 * taker(p) + 1) * HD, HD)
        out_ref[p, 0] = k_ref[:, at]
        out_ref[p, 1] = quarters(v_ref[:, at])
        out_ref[p, 2] = q_ref[:rows, at]
        out_ref[p, 3] = q_ref[rows:, at]


def first_pack(queries, keys, values):
    rows, width = keys.shape[0] // 2, keys.shape[1]
    half = pl.BlockSpec((rows, width), lambda i: (0, 0))
    return pl.pallas_call(
        first_pack_kernel,
        grid=(1,),
        in_specs=[pl.BlockSpec(queries.shape, lambda i: (0, 0)), half, half],
        out_specs=pl.BlockSpec((8, 4, rows, HD), lambda i: (0, 0, 0, 0)),
        out_shape=jax.ShapeDtypeStruct((8, 4, rows, HD), jnp.bfloat16),
        compiler_params=params(),
        cost_estimate=estimate(3),
        name="pack_first",
    )(queries, keys, values)


def pack_kernel(q_ref, k_ref, v_ref, b_ref, lin_ref):
    half = b_ref.shape[2]
    for n in range(2):
        b_ref[n, 0] = k_ref[half:, (2 * n + 1) * HD : (2 * n + 2) * HD]
        b_ref[n, 1] = quarters(v_ref[half:, (2 * n + 1) * HD : (2 * n + 2) * HD])
        for m, ref in enumerate((q_ref, k_ref, v_ref)):
            lin_ref[n, m] = ref[:, 2 * n * HD : (2 * n + 1) * HD]


def pack(queries, keys, values):
    tokens = keys.shape[0]
    spec = pl.BlockSpec((tokens, 4 * HD), lambda j: (0, j))
    shapes = [(2, 4, 2, tokens // 2, HD), (2, 4, 3, tokens, HD)]
    out = pl.pallas_call(
        pack_kernel,
        grid=(4,),
        in_specs=[spec, spec, spec],
        out_specs=[pl.BlockSpec((2, None) + shape[2:], lambda j: (0, j, 0, 0, 0)) for shape in shapes],
        out_shape=[jax.ShapeDtypeStruct(shape, jnp.bfloat16) for shape in shapes],
        compiler_params=params(),
        cost_estimate=estimate(5),
        name="pack_rest",
    )(queries, keys, values)
    return [a.reshape((8,) + a.shape[2:]) for a in out]


def own_kernel(first, q_ref, kv_ref, *refs):
    if first:
        acc_ref, k_ref, v_ref = refs
    else:
        acc_in, acc_ref, k_ref, v_ref = refs
    sources, _, rows, width = kv_ref.shape
    for p in range(sources):
        place(kv_ref[p, 0], kv_ref[p, 1], k_ref, v_ref, p * rows)
    key = lax.broadcasted_iota(jnp.int32, (rows, 2 * rows), 0)
    query = lax.broadcasted_iota(jnp.int32, (rows, 2 * rows), 1)
    causal = key + (0 if first else rows) <= query
    for i in range(sources):
        columns = slice(i * 2 * rows, (i + 1) * 2 * rows)
        q = scaled(q_ref[i].reshape(2 * rows, width))
        s = jnp.where(causal, dot_t(k_ref[i * rows : (i + 1) * rows, :], q), NEGATIVE)
        m = jnp.max(s, axis=0, keepdims=True)
        if not first:
            old = acc_in[TOP : TOP + 1, columns]
            m = jnp.maximum(old, m)
        if i:
            before = dot_t(k_ref[: i * rows, :], q)
            m = jnp.maximum(m, jnp.max(before, axis=0, keepdims=True))
        prob = jnp.exp2(s - m).astype(jnp.bfloat16)
        acc = jnp.dot(v_ref[:, i * rows : (i + 1) * rows], prob, preferred_element_type=jnp.float32)
        if i:
            prob = jnp.exp2(before - m).astype(jnp.bfloat16)
            acc += jnp.dot(v_ref[:, : i * rows], prob, preferred_element_type=jnp.float32)
        if not first:
            acc += acc_in[:TOP, columns] * jnp.exp2(old - m)
        acc_ref[:TOP, columns] = acc
        acc_ref[TOP:, columns] = jnp.broadcast_to(m, (8, 2 * rows))


def own_block(q, kv, acc=None):
    sources, _, rows, width = q.shape
    tokens = sources * rows * 2
    acc_spec = pl.BlockSpec((TOP + 8, tokens), lambda i: (0, 0))
    return pl.pallas_call(
        functools.partial(own_kernel, acc is None),
        grid=(1,),
        in_specs=[
            pl.BlockSpec((sources, 2, rows, width), lambda i: (0, 1, 0, 0)),
            pl.BlockSpec((sources, 2, rows, width), lambda i: (0, 0, 0, 0)),
        ]
        + ([] if acc is None else [acc_spec]),
        out_specs=acc_spec,
        scratch_shapes=[
            pltpu.VMEM((tokens // 2, 2 * width), jnp.bfloat16),
            pltpu.VMEM((TOP, tokens // 2), jnp.bfloat16),
        ],
        out_shape=jax.ShapeDtypeStruct((TOP + 8, tokens), jnp.float32),
        compiler_params=params(),
        cost_estimate=estimate(11),
        name="own_block",
    )(q, kv, *([] if acc is None else [acc]))


def half_of(pos_ref, away):
    return 1 - pos_ref[1] if away else pos_ref[1]


def takers(call):
    return [(z, call - 3 + z) for z, pairs in ((1, 2), (2, 4), (3, 5)) if 0 <= call - 3 + z < pairs]


def times_used(call, sel_ref, pos_ref):
    z = pos_ref[0]
    two = (sel_ref[3, 1] == 2) | (sel_ref[3, 2] == 2)
    both = two & ((sel_ref[3, 1] == 1) | (sel_ref[3, 2] == 1))
    block = -1
    for zz, pair in takers(call):
        if zz == 1:
            there = 0
        elif zz == 2:
            there = (1, 1, 0, 0)[pair]
        else:
            there = (2, jnp.where(two, 2, 1), 1, jnp.where(both, 1, 0), jnp.where(both, -1, 0))[pair]
        block = jnp.where(z == zz, there, block)
    return (sel_ref[z, 1] == block).astype(jnp.int32) + (sel_ref[z, 2] == block).astype(jnp.int32)


def place_chunks(call, pos_ref, chunks, chunk_ref, sem, k_ref, v_ref):
    for n, (z, _) in enumerate(takers(call)):

        @pl.when(pos_ref[0] == z)
        def _():
            copies = [
                pltpu.make_async_copy(chunks[2 * n + i], chunk_ref.at[i], sem.at[i]) for i in range(2)
            ]
            for copy in copies:
                copy.start()
            for copy in copies:
                copy.wait()

    _, sources, _, rows, _ = chunk_ref.shape
    for n in range(2):
        for p in range(sources):
            place(chunk_ref[n, p, 0], chunk_ref[n, p, 1], k_ref, v_ref, (n * sources + p) * rows)


def folded(q, count, acc, old, k_ref, v_ref):
    s = dot_t(k_ref[...], scaled(q.reshape(-1, HD)))
    m = jnp.maximum(old, jnp.max(s, axis=0, keepdims=True))
    prob = jnp.exp2(s - m).astype(jnp.bfloat16)
    acc = acc * jnp.exp2(old - m) + count.astype(jnp.float32) * jnp.dot(
        v_ref[...], prob, preferred_element_type=jnp.float32
    )
    return acc, m


def fold_kernel(call, sel_ref, pos_ref, q_ref, *refs):
    n = 2 * len(takers(call))
    chunks, (acc_in, acc_out, k_ref, v_ref, chunk_ref, chunk_sem, acc_ref, sem) = refs[:n], refs[n:]
    count = times_used(call, sel_ref, pos_ref)
    sources, _, rows, width = q_ref.shape
    half = sources * rows

    @pl.when(count > 0)
    def _():
        def copies(out):
            for h in range(2):
                part = pl.ds(h * half, half)
                there, here = (acc_out if out else acc_in).at[:, part], acc_ref.at[h]
                yield pltpu.make_async_copy(*((here, there) if out else (there, here)), sem.at[2 * out + h])

        fetch, store = list(copies(0)), list(copies(1))
        for copy in fetch:
            copy.start()
        place_chunks(call, pos_ref, chunks, chunk_ref, chunk_sem, k_ref, v_ref)
        for h in range(2):
            fetch[h].wait()
            q = q_ref[h * sources // 2 : (h + 1) * sources // 2]
            acc, m = folded(q, count, acc_ref[h, :TOP], acc_ref[h, TOP : TOP + 1], k_ref, v_ref)
            acc_ref[h, :TOP] = acc
            acc_ref[h, TOP:] = jnp.broadcast_to(m, (8, half))
            store[h].start()
        for copy in store:
            copy.wait()


def chunk_scratch(chunk):
    keys = 2 * chunk.shape[0] * chunk.shape[2]
    return [
        pltpu.VMEM((keys, 2 * HD), jnp.bfloat16),
        pltpu.VMEM((TOP, keys), jnp.bfloat16),
        pltpu.VMEM((2,) + chunk.shape, chunk.dtype),
        pltpu.SemaphoreType.DMA((2,)),
    ]


def call_chunks(call, got):
    return [got[2 * pair + i] for _, pair in takers(call) for i in range(2)]


def fold(call, selection, pos, q, got, acc):
    sources, _, rows, width = q.shape
    half = sources * rows
    chunks = call_chunks(call, got)
    anywhere = pl.BlockSpec(memory_space=pl.ANY)
    return pl.pallas_call(
        functools.partial(fold_kernel, call),
        grid_spec=pltpu.PrefetchScalarGridSpec(
            num_scalar_prefetch=2,
            grid=(1,),
            in_specs=[pl.BlockSpec((sources, 2, rows, width), lambda i, sel, pos: (0, 1, 0, 0))]
            + [anywhere] * (len(chunks) + 1),
            out_specs=anywhere,
            scratch_shapes=chunk_scratch(chunks[0])
            + [pltpu.VMEM((2, TOP + 8, half), jnp.float32), pltpu.SemaphoreType.DMA((4,))],
        ),
        out_shape=jax.ShapeDtypeStruct(acc.shape, acc.dtype),
        input_output_aliases={3 + len(chunks): 0},
        compiler_params=params(),
        cost_estimate=estimate(14),
        name="fold_chunks",
    )(selection, pos, q, *chunks, acc)


def last_kernel(call, sel_ref, pos_ref, q_ref, *refs):
    n = 2 * len(takers(call))
    chunks, (acc_ref, gain_ref, out_ref, k_ref, v_ref, chunk_ref, sem) = refs[:n], refs[n:]
    count = times_used(call, sel_ref, pos_ref)

    def finish(acc):
        out = acc[:HD] / acc[HD : HD + 1]
        out = out * lax.rsqrt(jnp.mean(out * out, axis=0, keepdims=True) + EPSILON)
        out_ref[...] = (out.T * gain_ref[...]).astype(jnp.bfloat16)

    @pl.when(count > 0)
    def _():
        place_chunks(call, pos_ref, chunks, chunk_ref, sem, k_ref, v_ref)
        finish(folded(q_ref[...], count, acc_ref[:TOP], acc_ref[TOP : TOP + 1], k_ref, v_ref)[0])

    @pl.when(count == 0)
    def _():
        finish(acc_ref[:TOP])


def fold_last(away, call, selection, pos, q, got, acc, gain):
    sources, _, rows, width = q.shape
    half = sources * rows
    chunks = call_chunks(call, got)
    return pl.pallas_call(
        functools.partial(last_kernel, call),
        grid_spec=pltpu.PrefetchScalarGridSpec(
            num_scalar_prefetch=2,
            grid=(1,),
            in_specs=[
                pl.BlockSpec((sources // 2, 2, rows, width), lambda i, sel, pos: (half_of(pos, away), 1, 0, 0)),
            ]
            + [pl.BlockSpec(memory_space=pl.ANY)] * len(chunks)
            + [
                pl.BlockSpec((TOP + 8, half), lambda i, sel, pos: (0, half_of(pos, away))),
                pl.BlockSpec((1, width), lambda i, sel, pos: (0, 0)),
            ],
            out_specs=pl.BlockSpec((half, width), lambda i, sel, pos: (0, 0)),
            scratch_shapes=chunk_scratch(chunks[0]),
        ),
        out_shape=jax.ShapeDtypeStruct((half, width), jnp.bfloat16),
        compiler_params=params(),
        cost_estimate=estimate(8),
        name="fold_last",
    )(selection, pos, q, *chunks, acc, gain)


def states_kernel(lin_ref, weight_ref, decay_ref, entering_ref, final_ref):
    spans = entering_ref.shape[0]
    state = jnp.zeros((HD, HD), jnp.float32)
    whole = jnp.ones((1, HD), jnp.float32)
    for s in range(spans):
        rows = pl.ds(s % SUB * CH, CH)
        entering_ref[s] = state
        k = lin_ref[s // SUB, 1, rows, :].astype(jnp.float32)
        v = lin_ref[s // SUB, 2, rows, :]
        weighted = (k * weight_ref[:, s : s + 1]).astype(jnp.bfloat16)
        inc = lax.dot_general(
            weighted, v, (((0,), (0,)), ((), ())), preferred_element_type=jnp.float32
        )
        state = decay_ref[s : s + 1, :] * state + inc
        whole = whole * decay_ref[s : s + 1, :]
    final_ref[:HD, :] = state
    final_ref[HD:, :] = jnp.broadcast_to(whole, (8, HD))


def states(lin, weight, decay):
    spans = decay.shape[0]
    return pl.pallas_call(
        states_kernel,
        out_shape=[
            jax.ShapeDtypeStruct((spans, HD, HD), jnp.float32),
            jax.ShapeDtypeStruct((HD + 8, HD), jnp.float32),
        ],
        compiler_params=params(),
        cost_estimate=estimate(2),
        name="span_states",
    )(lin, weight, decay)


def linear_kernel(lin_ref, entering_ref, one_ref, two_ref, three_ref, cum_ref, cum_t_ref, lead_ref, gain_ref, out_ref):
    carried = two_ref[:HD, :] + two_ref[HD : HD + 1, :] * three_ref[:HD, :]
    carried = one_ref[:HD, :] + one_ref[HD : HD + 1, :] * carried
    spans = entering_ref.shape[0]
    r = lax.broadcasted_iota(jnp.int32, (CH, CH), 0)
    c = lax.broadcasted_iota(jnp.int32, (CH, CH), 1)
    causal = c <= r
    for s in range(spans):
        rows = pl.ds(s % SUB * CH, CH)
        q, k, v = (lin_ref[s // SUB, n, rows, :] for n in range(3))
        column = cum_t_ref[:, s : s + 1]
        gap = jnp.where(causal, column - cum_ref[s : s + 1, :], 0.0)
        damping = jnp.where(causal, jnp.exp(gap), 0.0)
        mixing = (dot_t(q, k) * damping).astype(jnp.bfloat16)
        inside = jnp.dot(mixing, v, preferred_element_type=jnp.float32)
        state = entering_ref[s] + lead_ref[s : s + 1, :] * carried
        high = state.astype(jnp.bfloat16)
        low = (state - high.astype(jnp.float32)).astype(jnp.bfloat16)
        across = jnp.dot(q, jnp.concatenate([high, low], axis=1), preferred_element_type=jnp.float32)
        out = inside + jnp.exp(column) * (across[:, :HD] + across[:, HD:])
        out_ref[s * CH : (s + 1) * CH, :] = (normalize(out) * gain_ref[...]).astype(jnp.bfloat16)


def linear(lin, entering, finals, cum, cum_t, lead, gain):
    spans = cum.shape[0]
    return pl.pallas_call(
        linear_kernel,
        out_shape=jax.ShapeDtypeStruct((spans * CH, HD), jnp.bfloat16),
        compiler_params=params(),
        cost_estimate=estimate(5),
        name="linear_heads",
    )(lin, entering, *finals, cum, cum_t, lead, gain)


def paired_device(queries, keys, values, log_decay, selection, out_gain):
    z, x = lax.axis_index("z"), lax.axis_index("x")
    pos = jnp.stack([z, x]).astype(jnp.int32)

    def to_heads(parts):
        return lax.all_to_all(parts, ("x", "y", "c"), 0, 0, tiled=True)

    def after(a, *earlier):
        return lax.optimization_barrier((a,) + earlier)[0]

    front = to_heads(first_pack(queries, keys, values))
    part_b, lin_in = pack(queries, keys, values)
    own = [front[:, :2, i * QUARTER : (i + 1) * QUARTER] for i in range(2)]
    part_b = to_heads(after(part_b, *own))
    own += [part_b[:, :, i * QUARTER : (i + 1) * QUARTER] for i in range(2)]

    two = (selection[3, 1] == 2) | (selection[3, 2] == 2)
    both = two & ((selection[3, 1] == 1) | (selection[3, 2] == 1))
    early, late = (z == 2) & ~two, (z == 2) & ~both
    up = [(0, 1), (1, 2), (2, 3)]
    got, sent = [], []

    def go_up(*earlier):
        t = len(got)
        if t < 2:
            send = own[t]
        elif t < 4:
            send = jnp.where(early, got[t - 2], after(own[t], *earlier))
        elif t < 6:
            send = jnp.where(early, got[t - 2], after(got[t - 4], *earlier))
        elif t < 8:
            send = jnp.where(late, got[t - 2], after(got[t - 4], *earlier))
        else:
            send = after(got[t - 2], *earlier)
        sent.append(send)
        got.append(lax.ppermute(send, "z", up if t < 4 else up[1:] if t < 8 else up[2:]))

    def fold_pair(pair, acc, *earlier):
        return fold(pair, selection, pos, front, got, after(acc, *earlier))

    gains = lax.dynamic_slice_in_dim(out_gain, x * 2 * HD, 2 * HD).reshape(2, 1, HD)
    go_up()
    go_up()
    acc = own_block(front, front)
    go_up(acc)
    lin_in = to_heads(after(lin_in, sent[2]))
    go_up(acc)
    acc = own_block(front, part_b, after(acc, sent[3]))
    go_up(acc)
    acc = fold_pair(0, acc, sent[4])
    go_up(acc)
    go_up(acc)
    acc = fold_pair(1, acc, sent[5], sent[6])
    go_up(acc)

    swap = [(0, 1), (1, 0)]
    own_decay = lax.dynamic_index_in_dim(log_decay, x, 1, False)
    sent_decay = lax.dynamic_index_in_dim(log_decay, 1 - x, 1, False)
    got_decay = lax.ppermute(sent_decay, "x", swap)
    decays = jnp.where(x == 0, jnp.stack([own_decay, got_decay]), jnp.stack([got_decay, own_decay]))
    cum = jnp.cumsum(decays.reshape(-1, CH), axis=1)
    ending = cum[:, -1]
    spans = cum.shape[0]
    weight = jnp.exp(ending[:, None] - cum).T
    decay = jnp.broadcast_to(jnp.exp(ending)[:, None], (spans, HD))
    lead = jnp.broadcast_to(jnp.exp(jnp.cumsum(ending) - ending)[:, None], (spans, HD))
    entering, final = states(after(lin_in, sent[7], acc), weight, decay)
    go_up()
    finals = [lax.ppermute(final, "z", pairs) for pairs in (up, [(0, 2), (1, 3)], [(0, 3)])]
    acc = fold_pair(2, acc, final)
    go_up(acc)
    acc = fold_pair(3, acc, sent[9])
    entering = after(entering, acc)
    lin = linear(lin_in, entering, finals, cum, cum.T, lead, gains[0])
    rows = lin.shape[0] // 2
    lin_own = lax.dynamic_slice_in_dim(lin, x * rows, rows)
    lin_got = lax.ppermute(lax.dynamic_slice_in_dim(lin, (1 - x) * rows, rows), "x", swap)

    acc = after(acc, lin)
    att_away = fold_last(True, 4, selection, pos, front, got, acc, gains[1])
    att_got = lax.ppermute(att_away, "x", swap)
    att_own = fold_last(False, 4, selection, pos, front, got, acc, gains[1])
    return jnp.where(
        x == 0,
        jnp.concatenate([lin_own, att_own, lin_got, att_got], axis=1),
        jnp.concatenate([lin_got, att_got, lin_own, att_own], axis=1),
    )


def solution(mesh):
    args = (P(("seq", "head"), None),) * 3 + (P("seq", "head"), P(), P("head"))
    if mesh.shape["seq"] == 8 and mesh.shape["head"] == 4:
        fine = jax.sharding.Mesh(mesh.devices.reshape(4, 2, 2, 2), ("z", "x", "y", "c"))
        everywhere = P(("z", "x", "y", "c"), None)
        return jax.shard_map(
            paired_device,
            mesh=fine,
            in_specs=(everywhere,) * 3 + (P(("z", "x"), ("y", "c")), P(), P(("y", "c"))),
            out_specs=P(("z", "x"), ("y", "c")),
            check_vma=False,
        )
    return jax.shard_map(
        per_device, mesh=mesh, in_specs=args, out_specs=P("seq", "head"), check_vma=False
    )
```

```python
import functools

import jax
import jax.numpy as jnp
from jax import lax
from jax.experimental import pallas as pl
from jax.experimental.pallas import tpu as pltpu
from jax.sharding import PartitionSpec as P

HD = 128
BLK = 4096
TILE = 1024
CH = 128


EPSILON = 1e-06
NEGATIVE = -1e30
HIGHEST = lax.Precision.HIGHEST
VMEM_LIMIT = 56 << 20


def carried_in(part, axis, combine, identity):
    place = lax.axis_index(axis)
    gathered = jax.tree.map(lambda a: lax.all_gather(a, axis), part)
    state = jax.tree.map(lambda a, e: jnp.zeros_like(a) + jnp.asarray(e, a.dtype), part, identity)

    def one(turn, state):
        return combine(
            state, jax.tree.map(lambda a: lax.dynamic_index_in_dim(a, turn, 0, False), gathered)
        )

    return lax.fori_loop(0, place, one, state)


def within_spans(query_lin, key_lin, value_lin, log_decay, span):
    rows, record_entries, width = query_lin.shape
    count = rows // span
    probe_segments = query_lin.reshape(count, span, record_entries, width)
    key_spans = key_lin.reshape(count, span, record_entries, width)
    value_spans = value_lin.reshape(count, span, record_entries, width)
    running = jnp.cumsum(log_decay.reshape(count, span, record_entries), axis=1)
    by_line = jnp.transpose(running, (0, 2, 1))
    causal = jnp.arange(span)[:, None] >= jnp.arange(span)[None, :]
    stride_gap = jnp.where(causal, by_line[:, :, :, None] - by_line[:, :, None, :], 0.0)
    damping = jnp.where(causal, jnp.exp(stride_gap), 0.0)
    scores = jnp.einsum(
        "ctld,csld->clts", probe_segments, key_spans, preferred_element_type=jnp.float32
    )
    mixing = (scores * damping).astype(jnp.bfloat16)
    inside = jnp.einsum("clts,csld->ctld", mixing, value_spans, preferred_element_type=jnp.float32)
    ending = running[:, -1, :]
    weighted_keys = (
        key_spans.astype(jnp.float32) * jnp.exp(ending[:, None, :] - running)[..., None]
    ).astype(jnp.bfloat16)
    increments = jnp.einsum(
        "ctld,ctle->clde", weighted_keys, value_spans, preferred_element_type=jnp.float32
    )

    def advance(state, inputs):
        decay_sum, increment = inputs
        return (jnp.exp(decay_sum)[:, None, None] * state + increment, state)

    final_state, entering = lax.scan(
        advance, jnp.zeros((record_entries, width, width), jnp.float32), (ending, increments)
    )
    weighted_queries = probe_segments.astype(jnp.float32) * jnp.exp(running)[..., None]
    across = jnp.einsum("ctld,clde->ctle", weighted_queries, entering, precision=HIGHEST)
    return (inside + across, weighted_queries, ending, final_state)


def attend_tiles(query, key_tiles, payload_blocks, query_pos, slot_open, per_slot):
    rows, record_entries, width = query.shape
    tile_len = key_tiles.shape[1]
    scale = width ** (-0.5)

    def tile_step(tile, carry):
        best, total, accum = carry
        slot = tile // per_slot
        key_pos = tile % per_slot * tile_len + jnp.arange(tile_len)
        key_tile = lax.dynamic_index_in_dim(key_tiles, tile, 0, keepdims=False)
        value_tile = lax.dynamic_index_in_dim(payload_blocks, tile, 0, keepdims=False)
        causal = key_pos[None, :] <= query_pos[:, None]
        allowed = jnp.where(slot == 0, causal, slot_open[slot])
        scores = (
            jnp.einsum("ild,jld->lij", query, key_tile, preferred_element_type=jnp.float32) * scale
        )
        masked = jnp.where(allowed[None], scores, NEGATIVE)
        tile_max = jnp.max(masked, axis=2)
        probs = jnp.where(allowed[None], jnp.exp(masked - tile_max[:, :, None]), 0.0).astype(
            jnp.bfloat16
        )
        tile_sum = jnp.sum(probs, axis=2, dtype=jnp.float32)
        tile_out = jnp.einsum("lij,jld->ild", probs, value_tile, preferred_element_type=jnp.float32)
        peak = jnp.maximum(best, tile_max)
        keep = jnp.exp(best - peak)
        fresh = jnp.exp(tile_max - peak)
        total = total * keep + tile_sum * fresh
        accum = accum * keep.T[:, :, None] + tile_out * fresh.T[:, :, None]
        return (peak, total, accum)

    start = (
        jnp.full((record_entries, rows), NEGATIVE, jnp.float32),
        jnp.zeros((record_entries, rows), jnp.float32),
        jnp.zeros((rows, record_entries, width), jnp.float32),
    )
    best, total, accum = lax.fori_loop(0, key_tiles.shape[0], tile_step, start)
    return accum / total.T[:, :, None]


def request_table(selection, group, seq_count):
    dest_block = jnp.arange(seq_count) // group
    chosen = jnp.take(selection, dest_block, axis=0)
    return jnp.transpose(chosen)[:, None, :] * group + jnp.arange(group)[None, :, None]


def normalize(heads):
    return heads * lax.rsqrt(jnp.mean(heads * heads, axis=-1, keepdims=True) + EPSILON)


def per_device(queries, keys, values, log_decay, selection, out_gain):
    queries, keys, values = (
        lax.all_to_all(queries, "head", split_axis=1, concat_axis=0, tiled=True),
        lax.all_to_all(keys, "head", split_axis=1, concat_axis=0, tiled=True),
        lax.all_to_all(values, "head", split_axis=1, concat_axis=0, tiled=True),
    )
    rows = queries.shape[0]
    width = HD
    pairs = queries.shape[1] // (2 * width)
    query_pairs = queries.reshape(rows, pairs, 2, width)
    paired_keys = keys.reshape(rows, pairs, 2, width)
    paired_values = values.reshape(rows, pairs, 2, width)
    linear_part, weighted_queries, ending, final_state = within_spans(
        query_pairs[:, :, 0], paired_keys[:, :, 0], paired_values[:, :, 0], log_decay, CH
    )
    total_decay = jnp.sum(ending, axis=0)

    def chain(earlier, later):
        return (earlier[0] + later[0], jnp.exp(later[0])[:, None, None] * earlier[1] + later[1])

    leading_decay, carried = carried_in(
        (total_decay, final_state),
        "seq",
        chain,
        (jnp.zeros_like(total_decay), jnp.zeros_like(final_state)),
    )
    span_start = jnp.cumsum(ending, axis=0) - ending
    shifted = weighted_queries * jnp.exp(span_start)[:, None, :, None]
    correction = jnp.einsum("ctld,lde->ctle", shifted, carried, precision=HIGHEST)
    linear_out = (linear_part + correction).reshape(rows, pairs, width)
    seq_count = lax.axis_size("seq")
    position = lax.axis_index("seq")
    group = BLK // rows
    block_index = position // group
    rank = position % group
    piece_rows = rows // seq_count
    query_moba = query_pairs[:, :, 1]
    key_moba = paired_keys[:, :, 1]
    value_moba = paired_values[:, :, 1]
    spread_keys, spread_values = (
        lax.all_to_all(
            key_moba.reshape(seq_count, piece_rows, pairs, width),
            "seq",
            split_axis=0,
            concat_axis=0,
            tiled=True,
        ),
        lax.all_to_all(
            value_moba.reshape(seq_count, piece_rows, pairs, width),
            "seq",
            split_axis=0,
            concat_axis=0,
            tiled=True,
        ),
    )
    table = request_table(selection, group, seq_count)
    block_keys, block_values = (
        lax.all_to_all(
            jnp.take(spread_keys, table, axis=0), "seq", split_axis=2, concat_axis=2, tiled=True
        ),
        lax.all_to_all(
            jnp.take(spread_values, table, axis=0), "seq", split_axis=2, concat_axis=2, tiled=True
        ),
    )
    block_keys = block_keys.reshape(3, BLK, pairs, width)
    block_values = block_values.reshape(3, BLK, pairs, width)
    per_slot = BLK // TILE
    key_tiles = block_keys.reshape(3 * per_slot, TILE, pairs, width)
    payload_blocks = block_values.reshape(3 * per_slot, TILE, pairs, width)
    chosen = jnp.take(selection, block_index, axis=0)
    slot_open = jnp.concatenate([jnp.ones((1,), jnp.bool_), chosen[1:] != block_index])
    query_pos = rank * rows + jnp.arange(rows)
    attended = attend_tiles(query_moba, key_tiles, payload_blocks, query_pos, slot_open, per_slot)
    both = jnp.stack([normalize(linear_out), normalize(attended)], axis=2).reshape(
        rows, pairs * 2 * width
    )
    return (both * out_gain[None, :]).astype(jnp.bfloat16)


SUB = 4
QUARTER = 128
SUMS = 16
TOP = HD + SUMS
SPEED = 2e7
LOG2E = 1.4426950408889634


def dot_t(a, b):
    return lax.dot_general(a, b, (((1,), (1,)), ((), ())), preferred_element_type=jnp.float32)


def scaled(q):
    wide = q.astype(jnp.float32) * (HD ** (-0.5) * LOG2E)
    high = wide.astype(jnp.bfloat16)
    return jnp.concatenate([high, (wide - high.astype(jnp.float32)).astype(jnp.bfloat16)], axis=1)


def place(k, v, k_ref, v_ref, at):
    rows = k.shape[0]
    k_ref[at : at + rows, :] = jnp.concatenate([k, k], axis=1)
    for i in range(0, rows, QUARTER):
        v_ref[:HD, at + i : at + i + QUARTER] = v[i : i + QUARTER, :]
    v_ref[HD:, at : at + rows] = jnp.ones((SUMS, rows), jnp.bfloat16)


def quarters(v):
    return jnp.concatenate([v[i : i + QUARTER].T for i in range(0, v.shape[0], QUARTER)], axis=0)


def estimate(us, transcendentals=0):
    return pl.CostEstimate(flops=int(us * SPEED), bytes_accessed=1 << 20, transcendentals=transcendentals)


def params(limit=VMEM_LIMIT):
    return pltpu.CompilerParams(vmem_limit_bytes=limit)


def taker(p):
    return 2 * (p % 4) + p // 4


def first_pack_kernel(q_ref, k_ref, v_ref, out_ref):
    rows = k_ref.shape[0]
    for p in range(8):
        at = pl.ds((2 * taker(p) + 1) * HD, HD)
        out_ref[p, 0] = k_ref[:, at]
        out_ref[p, 1] = quarters(v_ref[:, at])
        out_ref[p, 2] = q_ref[:rows, at]
        out_ref[p, 3] = q_ref[rows:, at]


def first_pack(queries, keys, values):
    rows, width = keys.shape[0] // 2, keys.shape[1]
    half = pl.BlockSpec((rows, width), lambda i: (0, 0))
    return pl.pallas_call(
        first_pack_kernel,
        grid=(1,),
        in_specs=[pl.BlockSpec(queries.shape, lambda i: (0, 0)), half, half],
        out_specs=pl.BlockSpec((8, 4, rows, HD), lambda i: (0, 0, 0, 0)),
        out_shape=jax.ShapeDtypeStruct((8, 4, rows, HD), jnp.bfloat16),
        compiler_params=params(),
        cost_estimate=estimate(3),
        name="pack_first",
    )(queries, keys, values)


def pack_kernel(q_ref, k_ref, v_ref, b_ref, kv_ref, q_out):
    half = b_ref.shape[2]
    for n in range(2):
        b_ref[n, 0] = k_ref[half:, (2 * n + 1) * HD : (2 * n + 2) * HD]
        b_ref[n, 1] = quarters(v_ref[half:, (2 * n + 1) * HD : (2 * n + 2) * HD])
        for m, ref in enumerate((k_ref, v_ref)):
            kv_ref[n, m] = ref[:, 2 * n * HD : (2 * n + 1) * HD]
        q_out[n] = q_ref[:, 2 * n * HD : (2 * n + 1) * HD]


def pack(queries, keys, values):
    tokens = keys.shape[0]
    spec = pl.BlockSpec((tokens, 4 * HD), lambda j: (0, j))
    shapes = [(2, 4, 2, tokens // 2, HD), (2, 4, 2, tokens, HD), (2, 4, tokens, HD)]
    out = pl.pallas_call(
        pack_kernel,
        grid=(4,),
        in_specs=[spec, spec, spec],
        out_specs=[pl.BlockSpec((2, None) + shape[2:], lambda j, n=len(shape): (0, j) + (0,) * (n - 2)) for shape in shapes],
        out_shape=[jax.ShapeDtypeStruct(shape, jnp.bfloat16) for shape in shapes],
        compiler_params=params(),
        cost_estimate=estimate(5),
        name="pack_rest",
    )(queries, keys, values)
    return [a.reshape((8,) + a.shape[2:]) for a in out]


def own_kernel(first, q_ref, kv_ref, *refs):
    if first:
        acc_ref, k_ref, v_ref = refs
    else:
        acc_in, acc_ref, k_ref, v_ref = refs
    sources, _, rows, width = kv_ref.shape
    for p in range(sources):
        place(kv_ref[p, 0], kv_ref[p, 1], k_ref, v_ref, p * rows)
    key = lax.broadcasted_iota(jnp.int32, (rows, 2 * rows), 0)
    query = lax.broadcasted_iota(jnp.int32, (rows, 2 * rows), 1)
    causal = key + (0 if first else rows) <= query
    for i in range(sources):
        columns = slice(i * 2 * rows, (i + 1) * 2 * rows)
        q = scaled(q_ref[i].reshape(2 * rows, width))
        s = jnp.where(causal, dot_t(k_ref[i * rows : (i + 1) * rows, :], q), NEGATIVE)
        m = jnp.max(s, axis=0, keepdims=True)
        if not first:
            old = acc_in[TOP : TOP + 1, columns]
            m = jnp.maximum(old, m)
        if i:
            before = dot_t(k_ref[: i * rows, :], q)
            m = jnp.maximum(m, jnp.max(before, axis=0, keepdims=True))
        prob = jnp.exp2(s - m).astype(jnp.bfloat16)
        acc = jnp.dot(v_ref[:, i * rows : (i + 1) * rows], prob, preferred_element_type=jnp.float32)
        if i:
            prob = jnp.exp2(before - m).astype(jnp.bfloat16)
            acc += jnp.dot(v_ref[:, : i * rows], prob, preferred_element_type=jnp.float32)
        if not first:
            acc += acc_in[:TOP, columns] * jnp.exp2(old - m)
        acc_ref[:TOP, columns] = acc
        acc_ref[TOP:, columns] = jnp.broadcast_to(m, (8, 2 * rows))


def own_block(q, kv, acc=None):
    sources, _, rows, width = q.shape
    tokens = sources * rows * 2
    acc_spec = pl.BlockSpec((TOP + 8, tokens), lambda i: (0, 0))
    return pl.pallas_call(
        functools.partial(own_kernel, acc is None),
        grid=(1,),
        in_specs=[
            pl.BlockSpec((sources, 2, rows, width), lambda i: (0, 1, 0, 0)),
            pl.BlockSpec((sources, 2, rows, width), lambda i: (0, 0, 0, 0)),
        ]
        + ([] if acc is None else [acc_spec]),
        out_specs=acc_spec,
        scratch_shapes=[
            pltpu.VMEM((tokens // 2, 2 * width), jnp.bfloat16),
            pltpu.VMEM((TOP, tokens // 2), jnp.bfloat16),
        ],
        out_shape=jax.ShapeDtypeStruct((TOP + 8, tokens), jnp.float32),
        compiler_params=params(),
        cost_estimate=estimate(11),
        name="own_block",
    )(q, kv, *([] if acc is None else [acc]))


def half_of(pos_ref, away):
    return 1 - pos_ref[1] if away else pos_ref[1]


def chosen(sel_ref):
    two = (sel_ref[3, 1] == 2) | (sel_ref[3, 2] == 2)
    return two, two & ((sel_ref[3, 1] == 1) | (sel_ref[3, 2] == 1))


def chunk_now(call, sel_ref, pos_ref):
    two, both = chosen(sel_ref)
    return (pos_ref[0] == 3) & ((~two | ~both) if call > 2 else ~two)


def times_used(call, sel_ref, pos_ref):
    z = pos_ref[0]
    two, both = chosen(sel_ref)

    def third(step):
        return (2, jnp.where(two, 2, 1), 1, jnp.where(both, 1, 0), jnp.where(both, -1, 0))[step]

    before = jnp.where(
        z == 1, (0, 0, -1, -1)[call - 1], jnp.where(z == 2, (1, 1, 0, 0)[call - 1], third(call - 1))
    )
    block = jnp.where(chunk_now(call, sel_ref, pos_ref), third(call), before)
    block = jnp.where(z == 0, -1, block)
    return (sel_ref[z, 1] == block).astype(jnp.int32) + (sel_ref[z, 2] == block).astype(jnp.int32)


def place_chunks(call, sel_ref, pos_ref, chunks, chunk_ref, sem, k_ref, v_ref):
    now = chunk_now(call, sel_ref, pos_ref)
    for n, cond in enumerate((~now, now)):

        @pl.when(cond)
        def _():
            copy = pltpu.make_async_copy(chunks[n], chunk_ref, sem)
            copy.start()
            copy.wait()

    sources, _, rows, _ = chunk_ref.shape
    for p in range(sources):
        place(chunk_ref[p, 0], chunk_ref[p, 1], k_ref, v_ref, p * rows)


def folded(q, count, acc, old, k_ref, v_ref):
    s = dot_t(k_ref[...], scaled(q.reshape(-1, HD)))
    m = jnp.maximum(old, jnp.max(s, axis=0, keepdims=True))
    prob = jnp.exp2(s - m).astype(jnp.bfloat16)
    acc = acc * jnp.exp2(old - m) + count.astype(jnp.float32) * jnp.dot(
        v_ref[...], prob, preferred_element_type=jnp.float32
    )
    return acc, m


def fold_kernel(call, sel_ref, pos_ref, q_ref, *refs):
    n = 2
    chunks, (acc_in, acc_out, k_ref, v_ref, chunk_ref, chunk_sem, acc_ref, sem) = refs[:n], refs[n:]
    count = times_used(call, sel_ref, pos_ref)
    sources, _, rows, width = q_ref.shape
    half = sources * rows

    @pl.when(count > 0)
    def _():
        def copies(out):
            for h in range(2):
                part = pl.ds(h * half, half)
                there, here = (acc_out if out else acc_in).at[:, part], acc_ref.at[h]
                yield pltpu.make_async_copy(*((here, there) if out else (there, here)), sem.at[2 * out + h])

        fetch, store = list(copies(0)), list(copies(1))
        for copy in fetch:
            copy.start()
        place_chunks(call, sel_ref, pos_ref, chunks, chunk_ref, chunk_sem, k_ref, v_ref)
        for h in range(2):
            fetch[h].wait()
            q = q_ref[h * sources // 2 : (h + 1) * sources // 2]
            acc, m = folded(q, count, acc_ref[h, :TOP], acc_ref[h, TOP : TOP + 1], k_ref, v_ref)
            acc_ref[h, :TOP] = acc
            acc_ref[h, TOP:] = jnp.broadcast_to(m, (8, half))
            store[h].start()
        for copy in store:
            copy.wait()


def chunk_scratch(chunk):
    keys = chunk.shape[0] * chunk.shape[2]
    return [
        pltpu.VMEM((keys, 2 * HD), jnp.bfloat16),
        pltpu.VMEM((TOP, keys), jnp.bfloat16),
        pltpu.VMEM(chunk.shape, chunk.dtype),
        pltpu.SemaphoreType.DMA,
    ]


def call_chunks(call, got):
    return got[call - 1 : call + 1]


def fold(call, selection, pos, q, got, acc):
    sources, _, rows, width = q.shape
    half = sources * rows
    chunks = call_chunks(call, got)
    anywhere = pl.BlockSpec(memory_space=pl.ANY)
    return pl.pallas_call(
        functools.partial(fold_kernel, call),
        grid_spec=pltpu.PrefetchScalarGridSpec(
            num_scalar_prefetch=2,
            grid=(1,),
            in_specs=[pl.BlockSpec((sources, 2, rows, width), lambda i, sel, pos: (0, 1, 0, 0))]
            + [anywhere] * (len(chunks) + 1),
            out_specs=anywhere,
            scratch_shapes=chunk_scratch(chunks[0])
            + [pltpu.VMEM((2, TOP + 8, half), jnp.float32), pltpu.SemaphoreType.DMA((4,))],
        ),
        out_shape=jax.ShapeDtypeStruct(acc.shape, acc.dtype),
        input_output_aliases={3 + len(chunks): 0},
        compiler_params=params(),
        cost_estimate=estimate(14),
        name="fold_chunks",
    )(selection, pos, q, *chunks, acc)


def last_kernel(call, sel_ref, pos_ref, q_ref, *refs):
    n = 2
    chunks, (acc_ref, gain_ref, out_ref, k_ref, v_ref, chunk_ref, sem) = refs[:n], refs[n:]
    count = times_used(call, sel_ref, pos_ref)

    def finish(acc):
        out = acc[:HD] / acc[HD : HD + 1]
        out = out * lax.rsqrt(jnp.mean(out * out, axis=0, keepdims=True) + EPSILON)
        out_ref[...] = (out.T * gain_ref[...]).astype(jnp.bfloat16)

    @pl.when(count > 0)
    def _():
        place_chunks(call, sel_ref, pos_ref, chunks, chunk_ref, sem, k_ref, v_ref)
        finish(folded(q_ref[...], count, acc_ref[:TOP], acc_ref[TOP : TOP + 1], k_ref, v_ref)[0])

    @pl.when(count == 0)
    def _():
        finish(acc_ref[:TOP])


def fold_last(away, call, selection, pos, q, got, acc, gain):
    sources, _, rows, width = q.shape
    half = sources * rows
    chunks = call_chunks(call, got)
    return pl.pallas_call(
        functools.partial(last_kernel, call),
        grid_spec=pltpu.PrefetchScalarGridSpec(
            num_scalar_prefetch=2,
            grid=(1,),
            in_specs=[
                pl.BlockSpec((sources // 2, 2, rows, width), lambda i, sel, pos: (half_of(pos, away), 1, 0, 0)),
            ]
            + [pl.BlockSpec(memory_space=pl.ANY)] * len(chunks)
            + [
                pl.BlockSpec((TOP + 8, half), lambda i, sel, pos: (0, half_of(pos, away))),
                pl.BlockSpec((1, width), lambda i, sel, pos: (0, 0)),
            ],
            out_specs=pl.BlockSpec((half, width), lambda i, sel, pos: (0, 0)),
            scratch_shapes=chunk_scratch(chunks[0]),
        ),
        out_shape=jax.ShapeDtypeStruct((half, width), jnp.bfloat16),
        compiler_params=params(),
        cost_estimate=estimate(8),
        name="fold_last",
    )(selection, pos, q, *chunks, acc, gain)


def states_kernel(kv_ref, weight_ref, decay_ref, entering_ref, final_ref):
    spans = entering_ref.shape[0]
    state = jnp.zeros((HD, HD), jnp.float32)
    whole = jnp.ones((1, HD), jnp.float32)
    for s in range(spans):
        rows = pl.ds(s % SUB * CH, CH)
        entering_ref[s] = state
        k = kv_ref[s // SUB, 0, rows, :].astype(jnp.float32)
        v = kv_ref[s // SUB, 1, rows, :]
        weighted = (k * weight_ref[:, s : s + 1]).astype(jnp.bfloat16)
        inc = lax.dot_general(
            weighted, v, (((0,), (0,)), ((), ())), preferred_element_type=jnp.float32
        )
        state = decay_ref[s : s + 1, :] * state + inc
        whole = whole * decay_ref[s : s + 1, :]
    final_ref[:HD, :] = state
    final_ref[HD:, :] = jnp.broadcast_to(whole, (8, HD))


def states(kv, weight, decay):
    spans = decay.shape[0]
    return pl.pallas_call(
        states_kernel,
        out_shape=[
            jax.ShapeDtypeStruct((spans, HD, HD), jnp.float32),
            jax.ShapeDtypeStruct((HD + 8, HD), jnp.float32),
        ],
        compiler_params=params(),
        cost_estimate=estimate(2),
        name="span_states",
    )(kv, weight, decay)


def linear_kernel(q_ref, kv_ref, entering_ref, one_ref, two_ref, three_ref, cum_ref, cum_t_ref, lead_ref, gain_ref, out_ref):
    carried = two_ref[:HD, :] + two_ref[HD : HD + 1, :] * three_ref[:HD, :]
    carried = one_ref[:HD, :] + one_ref[HD : HD + 1, :] * carried
    spans = entering_ref.shape[0]
    r = lax.broadcasted_iota(jnp.int32, (CH, CH), 0)
    c = lax.broadcasted_iota(jnp.int32, (CH, CH), 1)
    causal = c <= r
    for s in range(spans):
        rows = pl.ds(s % SUB * CH, CH)
        q = q_ref[s // SUB, rows, :]
        k, v = (kv_ref[s // SUB, n, rows, :] for n in range(2))
        column = cum_t_ref[:, s : s + 1]
        gap = jnp.where(causal, column - cum_ref[s : s + 1, :], 0.0)
        damping = jnp.where(causal, jnp.exp(gap), 0.0)
        mixing = (dot_t(q, k) * damping).astype(jnp.bfloat16)
        inside = jnp.dot(mixing, v, preferred_element_type=jnp.float32)
        state = entering_ref[s] + lead_ref[s : s + 1, :] * carried
        high = state.astype(jnp.bfloat16)
        low = (state - high.astype(jnp.float32)).astype(jnp.bfloat16)
        across = jnp.dot(q, jnp.concatenate([high, low], axis=1), preferred_element_type=jnp.float32)
        out = inside + jnp.exp(column) * (across[:, :HD] + across[:, HD:])
        out_ref[s * CH : (s + 1) * CH, :] = (normalize(out) * gain_ref[...]).astype(jnp.bfloat16)


def linear(q, kv, entering, finals, cum, cum_t, lead, gain):
    spans = cum.shape[0]
    return pl.pallas_call(
        linear_kernel,
        out_shape=jax.ShapeDtypeStruct((spans * CH, HD), jnp.bfloat16),
        compiler_params=params(),
        cost_estimate=estimate(5),
        name="linear_heads",
    )(q, kv, entering, *finals, cum, cum_t, lead, gain)


def paired_device(queries, keys, values, log_decay, selection, out_gain):
    z, x = lax.axis_index("z"), lax.axis_index("x")
    pos = jnp.stack([z, x]).astype(jnp.int32)

    def to_heads(parts):
        return lax.all_to_all(parts, ("x", "y", "c"), 0, 0, tiled=True)

    def after(a, *earlier):
        return lax.optimization_barrier((a,) + earlier)[0]

    front = to_heads(first_pack(queries, keys, values))
    part_b, kv_lin, q_lin = pack(queries, keys, values)
    part_a = after(front, part_b)[:, :2]
    swap = [(0, 1), (1, 0)]
    own_decay = lax.dynamic_index_in_dim(log_decay, x, 1, False)
    sent_decay = lax.dynamic_index_in_dim(log_decay, 1 - x, 1, False)
    got_decay = lax.ppermute(sent_decay, "x", swap)
    part_b = to_heads(after(part_b, part_a, got_decay))
    two, both = chosen(selection)
    early, late = (z == 2) & ~two, (z == 2) & ~both
    up = [(0, 1), (1, 2), (2, 3)]
    got, sent = [], []

    def go_up(*earlier):
        t = len(got)
        if t == 0:
            send = part_a
        elif t < 3:
            send = jnp.where(early, got[t - 1], after((part_b, got[0])[t - 1], *earlier))
        elif t < 4:
            send = jnp.where(late, got[t - 1], after(got[t - 2], *earlier))
        else:
            send = after(got[t - 1], *earlier)
        sent.append(send)
        got.append(lax.ppermute(send, "z", up if t < 2 else up[1:] if t < 4 else up[2:]))

    def fold_in(call, acc, *earlier):
        return fold(call, selection, pos, front, got, after(acc, *earlier))

    gains = lax.dynamic_slice_in_dim(out_gain, x * 2 * HD, 2 * HD).reshape(2, 1, HD)
    go_up()
    acc = own_block(front, front)
    kv_lin = to_heads(after(kv_lin, acc))
    go_up(acc)
    acc = own_block(front, part_b, after(acc, sent[1]))
    decays = jnp.where(x == 0, jnp.stack([own_decay, got_decay]), jnp.stack([got_decay, own_decay]))
    cum = jnp.cumsum(decays.reshape(-1, CH), axis=1)
    ending = cum[:, -1]
    spans = cum.shape[0]
    weight = jnp.exp(ending[:, None] - cum).T
    decay = jnp.broadcast_to(jnp.exp(ending)[:, None], (spans, HD))
    lead = jnp.broadcast_to(jnp.exp(jnp.cumsum(ending) - ending)[:, None], (spans, HD))
    entering, final = states(after(kv_lin, acc), weight, decay)
    finals = [lax.ppermute(final, "z", pairs) for pairs in (up, [(0, 2), (1, 3)], [(0, 3)])]
    q_lin = to_heads(after(q_lin, final))
    go_up(acc, final, lead, cum)
    acc = fold_in(1, acc, sent[2])
    go_up(acc, *finals)
    acc = fold_in(2, acc, sent[3])
    go_up(acc)
    entering = after(entering, acc)
    lin = linear(q_lin, kv_lin, entering, finals, cum, cum.T, lead, gains[0])
    acc = fold_in(3, after(acc, lin))
    rows = lin.shape[0] // 2
    lin_own = lax.dynamic_slice_in_dim(lin, x * rows, rows)
    lin_got = lax.ppermute(lax.dynamic_slice_in_dim(lin, (1 - x) * rows, rows), "x", swap)

    att_away = fold_last(True, 4, selection, pos, front, got, acc, gains[1])
    att_got = lax.ppermute(att_away, "x", swap)
    att_own = fold_last(False, 4, selection, pos, front, got, acc, gains[1])
    return jnp.where(
        x == 0,
        jnp.concatenate([lin_own, att_own, lin_got, att_got], axis=1),
        jnp.concatenate([lin_got, att_got, lin_own, att_own], axis=1),
    )


def solution(mesh):
    args = (P(("seq", "head"), None),) * 3 + (P("seq", "head"), P(), P("head"))
    if mesh.shape["seq"] == 8 and mesh.shape["head"] == 4:
        fine = jax.sharding.Mesh(mesh.devices.reshape(4, 2, 2, 2), ("z", "x", "y", "c"))
        everywhere = P(("z", "x", "y", "c"), None)
        return jax.shard_map(
            paired_device,
            mesh=fine,
            in_specs=(everywhere,) * 3 + (P(("z", "x"), ("y", "c")), P(), P(("y", "c"))),
            out_specs=P(("z", "x"), ("y", "c")),
            check_vma=False,
        )
    return jax.shard_map(
        per_device, mesh=mesh, in_specs=args, out_specs=P("seq", "head"), check_vma=False
    )
```

```python
import functools

import jax
import jax.numpy as jnp
from jax import lax
from jax.experimental import pallas as pl
from jax.experimental.pallas import tpu as pltpu
from jax.sharding import PartitionSpec as P

HD = 128
BLK = 4096
TILE = 1024
CH = 128


EPSILON = 1e-06
NEGATIVE = -1e30
HIGHEST = lax.Precision.HIGHEST
VMEM_LIMIT = 56 << 20


def carried_in(part, axis, combine, identity):
    place = lax.axis_index(axis)
    gathered = jax.tree.map(lambda a: lax.all_gather(a, axis), part)
    state = jax.tree.map(lambda a, e: jnp.zeros_like(a) + jnp.asarray(e, a.dtype), part, identity)

    def one(turn, state):
        return combine(
            state, jax.tree.map(lambda a: lax.dynamic_index_in_dim(a, turn, 0, False), gathered)
        )

    return lax.fori_loop(0, place, one, state)


def within_spans(query_lin, key_lin, value_lin, log_decay, span):
    rows, record_entries, width = query_lin.shape
    count = rows // span
    probe_segments = query_lin.reshape(count, span, record_entries, width)
    key_spans = key_lin.reshape(count, span, record_entries, width)
    value_spans = value_lin.reshape(count, span, record_entries, width)
    running = jnp.cumsum(log_decay.reshape(count, span, record_entries), axis=1)
    by_line = jnp.transpose(running, (0, 2, 1))
    causal = jnp.arange(span)[:, None] >= jnp.arange(span)[None, :]
    stride_gap = jnp.where(causal, by_line[:, :, :, None] - by_line[:, :, None, :], 0.0)
    damping = jnp.where(causal, jnp.exp(stride_gap), 0.0)
    scores = jnp.einsum(
        "ctld,csld->clts", probe_segments, key_spans, preferred_element_type=jnp.float32
    )
    mixing = (scores * damping).astype(jnp.bfloat16)
    inside = jnp.einsum("clts,csld->ctld", mixing, value_spans, preferred_element_type=jnp.float32)
    ending = running[:, -1, :]
    weighted_keys = (
        key_spans.astype(jnp.float32) * jnp.exp(ending[:, None, :] - running)[..., None]
    ).astype(jnp.bfloat16)
    increments = jnp.einsum(
        "ctld,ctle->clde", weighted_keys, value_spans, preferred_element_type=jnp.float32
    )

    def advance(state, inputs):
        decay_sum, increment = inputs
        return (jnp.exp(decay_sum)[:, None, None] * state + increment, state)

    final_state, entering = lax.scan(
        advance, jnp.zeros((record_entries, width, width), jnp.float32), (ending, increments)
    )
    weighted_queries = probe_segments.astype(jnp.float32) * jnp.exp(running)[..., None]
    across = jnp.einsum("ctld,clde->ctle", weighted_queries, entering, precision=HIGHEST)
    return (inside + across, weighted_queries, ending, final_state)


def attend_tiles(query, key_tiles, payload_blocks, query_pos, slot_open, per_slot):
    rows, record_entries, width = query.shape
    tile_len = key_tiles.shape[1]
    scale = width ** (-0.5)

    def tile_step(tile, carry):
        best, total, accum = carry
        slot = tile // per_slot
        key_pos = tile % per_slot * tile_len + jnp.arange(tile_len)
        key_tile = lax.dynamic_index_in_dim(key_tiles, tile, 0, keepdims=False)
        value_tile = lax.dynamic_index_in_dim(payload_blocks, tile, 0, keepdims=False)
        causal = key_pos[None, :] <= query_pos[:, None]
        allowed = jnp.where(slot == 0, causal, slot_open[slot])
        scores = (
            jnp.einsum("ild,jld->lij", query, key_tile, preferred_element_type=jnp.float32) * scale
        )
        masked = jnp.where(allowed[None], scores, NEGATIVE)
        tile_max = jnp.max(masked, axis=2)
        probs = jnp.where(allowed[None], jnp.exp(masked - tile_max[:, :, None]), 0.0).astype(
            jnp.bfloat16
        )
        tile_sum = jnp.sum(probs, axis=2, dtype=jnp.float32)
        tile_out = jnp.einsum("lij,jld->ild", probs, value_tile, preferred_element_type=jnp.float32)
        peak = jnp.maximum(best, tile_max)
        keep = jnp.exp(best - peak)
        fresh = jnp.exp(tile_max - peak)
        total = total * keep + tile_sum * fresh
        accum = accum * keep.T[:, :, None] + tile_out * fresh.T[:, :, None]
        return (peak, total, accum)

    start = (
        jnp.full((record_entries, rows), NEGATIVE, jnp.float32),
        jnp.zeros((record_entries, rows), jnp.float32),
        jnp.zeros((rows, record_entries, width), jnp.float32),
    )
    best, total, accum = lax.fori_loop(0, key_tiles.shape[0], tile_step, start)
    return accum / total.T[:, :, None]


def request_table(selection, group, seq_count):
    dest_block = jnp.arange(seq_count) // group
    chosen = jnp.take(selection, dest_block, axis=0)
    return jnp.transpose(chosen)[:, None, :] * group + jnp.arange(group)[None, :, None]


def normalize(heads):
    return heads * lax.rsqrt(jnp.mean(heads * heads, axis=-1, keepdims=True) + EPSILON)


def per_device(queries, keys, values, log_decay, selection, out_gain):
    queries, keys, values = (
        lax.all_to_all(queries, "head", split_axis=1, concat_axis=0, tiled=True),
        lax.all_to_all(keys, "head", split_axis=1, concat_axis=0, tiled=True),
        lax.all_to_all(values, "head", split_axis=1, concat_axis=0, tiled=True),
    )
    rows = queries.shape[0]
    width = HD
    pairs = queries.shape[1] // (2 * width)
    query_pairs = queries.reshape(rows, pairs, 2, width)
    paired_keys = keys.reshape(rows, pairs, 2, width)
    paired_values = values.reshape(rows, pairs, 2, width)
    linear_part, weighted_queries, ending, final_state = within_spans(
        query_pairs[:, :, 0], paired_keys[:, :, 0], paired_values[:, :, 0], log_decay, CH
    )
    total_decay = jnp.sum(ending, axis=0)

    def chain(earlier, later):
        return (earlier[0] + later[0], jnp.exp(later[0])[:, None, None] * earlier[1] + later[1])

    leading_decay, carried = carried_in(
        (total_decay, final_state),
        "seq",
        chain,
        (jnp.zeros_like(total_decay), jnp.zeros_like(final_state)),
    )
    span_start = jnp.cumsum(ending, axis=0) - ending
    shifted = weighted_queries * jnp.exp(span_start)[:, None, :, None]
    correction = jnp.einsum("ctld,lde->ctle", shifted, carried, precision=HIGHEST)
    linear_out = (linear_part + correction).reshape(rows, pairs, width)
    seq_count = lax.axis_size("seq")
    position = lax.axis_index("seq")
    group = BLK // rows
    block_index = position // group
    rank = position % group
    piece_rows = rows // seq_count
    query_moba = query_pairs[:, :, 1]
    key_moba = paired_keys[:, :, 1]
    value_moba = paired_values[:, :, 1]
    spread_keys, spread_values = (
        lax.all_to_all(
            key_moba.reshape(seq_count, piece_rows, pairs, width),
            "seq",
            split_axis=0,
            concat_axis=0,
            tiled=True,
        ),
        lax.all_to_all(
            value_moba.reshape(seq_count, piece_rows, pairs, width),
            "seq",
            split_axis=0,
            concat_axis=0,
            tiled=True,
        ),
    )
    table = request_table(selection, group, seq_count)
    block_keys, block_values = (
        lax.all_to_all(
            jnp.take(spread_keys, table, axis=0), "seq", split_axis=2, concat_axis=2, tiled=True
        ),
        lax.all_to_all(
            jnp.take(spread_values, table, axis=0), "seq", split_axis=2, concat_axis=2, tiled=True
        ),
    )
    block_keys = block_keys.reshape(3, BLK, pairs, width)
    block_values = block_values.reshape(3, BLK, pairs, width)
    per_slot = BLK // TILE
    key_tiles = block_keys.reshape(3 * per_slot, TILE, pairs, width)
    payload_blocks = block_values.reshape(3 * per_slot, TILE, pairs, width)
    chosen = jnp.take(selection, block_index, axis=0)
    slot_open = jnp.concatenate([jnp.ones((1,), jnp.bool_), chosen[1:] != block_index])
    query_pos = rank * rows + jnp.arange(rows)
    attended = attend_tiles(query_moba, key_tiles, payload_blocks, query_pos, slot_open, per_slot)
    both = jnp.stack([normalize(linear_out), normalize(attended)], axis=2).reshape(
        rows, pairs * 2 * width
    )
    return (both * out_gain[None, :]).astype(jnp.bfloat16)


SUB = 4
QUARTER = 128
SUMS = 16
TOP = HD + SUMS
SPEED = 2e7
LOG2E = 1.4426950408889634


def dot_t(a, b):
    return lax.dot_general(a, b, (((1,), (1,)), ((), ())), preferred_element_type=jnp.float32)


def scaled(q):
    wide = q.astype(jnp.float32) * (HD ** (-0.5) * LOG2E)
    high = wide.astype(jnp.bfloat16)
    return jnp.concatenate([high, (wide - high.astype(jnp.float32)).astype(jnp.bfloat16)], axis=1)


def place(k, v, k_ref, v_ref, at):
    rows = k.shape[0]
    k_ref[at : at + rows, :] = jnp.concatenate([k, k], axis=1)
    for i in range(0, rows, QUARTER):
        v_ref[:HD, at + i : at + i + QUARTER] = v[i : i + QUARTER, :]
    v_ref[HD:, at : at + rows] = jnp.ones((SUMS, rows), jnp.bfloat16)


def quarters(v):
    return jnp.concatenate([v[i : i + QUARTER].T for i in range(0, v.shape[0], QUARTER)], axis=0)


def estimate(us, transcendentals=0):
    return pl.CostEstimate(flops=int(us * SPEED), bytes_accessed=1 << 20, transcendentals=transcendentals)


def params(limit=VMEM_LIMIT):
    return pltpu.CompilerParams(vmem_limit_bytes=limit)


def taker(p):
    return 2 * (p % 4) + p // 4


def first_pack_kernel(k_ref, v_ref, out_ref):
    for p in range(8):
        at = pl.ds((2 * taker(p) + 1) * HD, HD)
        out_ref[p, 0] = k_ref[:, at]
        out_ref[p, 1] = quarters(v_ref[:, at])


def first_pack(keys, values):
    rows, width = keys.shape[0] // 2, keys.shape[1]
    half = pl.BlockSpec((rows, width), lambda i: (0, 0))
    return pl.pallas_call(
        first_pack_kernel,
        grid=(1,),
        in_specs=[half, half],
        out_specs=pl.BlockSpec((8, 2, rows, HD), lambda i: (0, 0, 0, 0)),
        out_shape=jax.ShapeDtypeStruct((8, 2, rows, HD), jnp.bfloat16),
        compiler_params=params(),
        cost_estimate=estimate(3),
        name="pack_first",
    )(keys, values)


def pack_kernel(q_ref, k_ref, v_ref, b_ref, kv_ref, q_out):
    half = b_ref.shape[2]
    for n in range(2):
        b_ref[n, 0] = k_ref[half:, (2 * n + 1) * HD : (2 * n + 2) * HD]
        b_ref[n, 1] = quarters(v_ref[half:, (2 * n + 1) * HD : (2 * n + 2) * HD])
        for m in range(2):
            b_ref[n, 2 + m] = q_ref[m * half : (m + 1) * half, (2 * n + 1) * HD : (2 * n + 2) * HD]
        for m, ref in enumerate((k_ref, v_ref)):
            kv_ref[n, m] = ref[:, 2 * n * HD : (2 * n + 1) * HD]
        q_out[n] = q_ref[:, 2 * n * HD : (2 * n + 1) * HD]


def pack(queries, keys, values):
    tokens = keys.shape[0]
    spec = pl.BlockSpec((tokens, 4 * HD), lambda j: (0, j))
    shapes = [(2, 4, 4, tokens // 2, HD), (2, 4, 2, tokens, HD), (2, 4, tokens, HD)]
    out = pl.pallas_call(
        pack_kernel,
        grid=(4,),
        in_specs=[spec, spec, spec],
        out_specs=[pl.BlockSpec((2, None) + shape[2:], lambda j, n=len(shape): (0, j) + (0,) * (n - 2)) for shape in shapes],
        out_shape=[jax.ShapeDtypeStruct(shape, jnp.bfloat16) for shape in shapes],
        compiler_params=params(),
        cost_estimate=estimate(5),
        name="pack_rest",
    )(queries, keys, values)
    return [a.reshape((8,) + a.shape[2:]) for a in out]


def own_kernel(first, q_ref, kv_ref, *refs):
    if first:
        acc_ref, k_ref, v_ref = refs
    else:
        acc_in, acc_ref, k_ref, v_ref = refs
    sources, _, rows, width = kv_ref.shape
    for p in range(sources):
        place(kv_ref[p, 0], kv_ref[p, 1], k_ref, v_ref, p * rows)
    key = lax.broadcasted_iota(jnp.int32, (rows, 2 * rows), 0)
    query = lax.broadcasted_iota(jnp.int32, (rows, 2 * rows), 1)
    causal = key + (0 if first else rows) <= query
    for i in range(sources):
        columns = slice(i * 2 * rows, (i + 1) * 2 * rows)
        q = scaled(q_ref[i].reshape(2 * rows, width))
        s = jnp.where(causal, dot_t(k_ref[i * rows : (i + 1) * rows, :], q), NEGATIVE)
        m = jnp.max(s, axis=0, keepdims=True)
        if not first:
            old = acc_in[TOP : TOP + 1, columns]
            m = jnp.maximum(old, m)
        if i:
            before = dot_t(k_ref[: i * rows, :], q)
            m = jnp.maximum(m, jnp.max(before, axis=0, keepdims=True))
        prob = jnp.exp2(s - m).astype(jnp.bfloat16)
        acc = jnp.dot(v_ref[:, i * rows : (i + 1) * rows], prob, preferred_element_type=jnp.float32)
        if i:
            prob = jnp.exp2(before - m).astype(jnp.bfloat16)
            acc += jnp.dot(v_ref[:, : i * rows], prob, preferred_element_type=jnp.float32)
        if not first:
            acc += acc_in[:TOP, columns] * jnp.exp2(old - m)
        acc_ref[:TOP, columns] = acc
        acc_ref[TOP:, columns] = jnp.broadcast_to(m, (8, 2 * rows))


def own_block(q, kv, acc=None):
    sources, _, rows, width = q.shape
    tokens = sources * rows * 2
    acc_spec = pl.BlockSpec((TOP + 8, tokens), lambda i: (0, 0))
    return pl.pallas_call(
        functools.partial(own_kernel, acc is None),
        grid=(1,),
        in_specs=[
            pl.BlockSpec((sources, 2, rows, width), lambda i: (0, 1, 0, 0)),
            pl.BlockSpec((sources, 2, rows, width), lambda i: (0, 0, 0, 0)),
        ]
        + ([] if acc is None else [acc_spec]),
        out_specs=acc_spec,
        scratch_shapes=[
            pltpu.VMEM((tokens // 2, 2 * width), jnp.bfloat16),
            pltpu.VMEM((TOP, tokens // 2), jnp.bfloat16),
        ],
        out_shape=jax.ShapeDtypeStruct((TOP + 8, tokens), jnp.float32),
        compiler_params=params(),
        cost_estimate=estimate(11),
        name="own_block",
    )(q, kv, *([] if acc is None else [acc]))


def half_of(pos_ref, away):
    return 1 - pos_ref[1] if away else pos_ref[1]


def chosen(sel_ref):
    two = (sel_ref[3, 1] == 2) | (sel_ref[3, 2] == 2)
    return two, two & ((sel_ref[3, 1] == 1) | (sel_ref[3, 2] == 1))


def chunk_now(call, sel_ref, pos_ref):
    two, both = chosen(sel_ref)
    return (pos_ref[0] == 3) & ((~two | ~both) if call > 2 else ~two)


def times_used(call, sel_ref, pos_ref):
    z = pos_ref[0]
    two, both = chosen(sel_ref)

    def third(step):
        return (2, jnp.where(two, 2, 1), 1, jnp.where(both, 1, 0), jnp.where(both, -1, 0))[step]

    before = jnp.where(
        z == 1, (0, 0, -1, -1)[call - 1], jnp.where(z == 2, (1, 1, 0, 0)[call - 1], third(call - 1))
    )
    block = jnp.where(chunk_now(call, sel_ref, pos_ref), third(call), before)
    block = jnp.where(z == 0, -1, block)
    return (sel_ref[z, 1] == block).astype(jnp.int32) + (sel_ref[z, 2] == block).astype(jnp.int32)


def place_chunks(call, sel_ref, pos_ref, chunks, chunk_ref, sem, k_ref, v_ref):
    now = chunk_now(call, sel_ref, pos_ref)
    for n, cond in enumerate((~now, now)):

        @pl.when(cond)
        def _():
            copy = pltpu.make_async_copy(chunks[n], chunk_ref, sem)
            copy.start()
            copy.wait()

    sources, _, rows, _ = chunk_ref.shape
    for p in range(sources):
        place(chunk_ref[p, 0], chunk_ref[p, 1], k_ref, v_ref, p * rows)


def folded(q, count, acc, old, k_ref, v_ref):
    s = dot_t(k_ref[...], scaled(q.reshape(-1, HD)))
    m = jnp.maximum(old, jnp.max(s, axis=0, keepdims=True))
    prob = jnp.exp2(s - m).astype(jnp.bfloat16)
    acc = acc * jnp.exp2(old - m) + count.astype(jnp.float32) * jnp.dot(
        v_ref[...], prob, preferred_element_type=jnp.float32
    )
    return acc, m


def fold_kernel(call, sel_ref, pos_ref, q_ref, *refs):
    n = 2
    chunks, (acc_in, acc_out, k_ref, v_ref, chunk_ref, chunk_sem, acc_ref, sem) = refs[:n], refs[n:]
    count = times_used(call, sel_ref, pos_ref)
    sources, _, rows, width = q_ref.shape
    half = sources * rows

    @pl.when(count > 0)
    def _():
        def copies(out):
            for h in range(2):
                part = pl.ds(h * half, half)
                there, here = (acc_out if out else acc_in).at[:, part], acc_ref.at[h]
                yield pltpu.make_async_copy(*((here, there) if out else (there, here)), sem.at[2 * out + h])

        fetch, store = list(copies(0)), list(copies(1))
        for copy in fetch:
            copy.start()
        place_chunks(call, sel_ref, pos_ref, chunks, chunk_ref, chunk_sem, k_ref, v_ref)
        for h in range(2):
            fetch[h].wait()
            q = q_ref[h * sources // 2 : (h + 1) * sources // 2]
            acc, m = folded(q, count, acc_ref[h, :TOP], acc_ref[h, TOP : TOP + 1], k_ref, v_ref)
            acc_ref[h, :TOP] = acc
            acc_ref[h, TOP:] = jnp.broadcast_to(m, (8, half))
            store[h].start()
        for copy in store:
            copy.wait()


def chunk_scratch(chunk):
    keys = chunk.shape[0] * chunk.shape[2]
    return [
        pltpu.VMEM((keys, 2 * HD), jnp.bfloat16),
        pltpu.VMEM((TOP, keys), jnp.bfloat16),
        pltpu.VMEM(chunk.shape, chunk.dtype),
        pltpu.SemaphoreType.DMA,
    ]


def call_chunks(call, got):
    return got[call - 1 : call + 1]


def fold(call, selection, pos, q, got, acc):
    sources, _, rows, width = q.shape
    half = sources * rows
    chunks = call_chunks(call, got)
    anywhere = pl.BlockSpec(memory_space=pl.ANY)
    return pl.pallas_call(
        functools.partial(fold_kernel, call),
        grid_spec=pltpu.PrefetchScalarGridSpec(
            num_scalar_prefetch=2,
            grid=(1,),
            in_specs=[pl.BlockSpec((sources, 2, rows, width), lambda i, sel, pos: (0, 1, 0, 0))]
            + [anywhere] * (len(chunks) + 1),
            out_specs=anywhere,
            scratch_shapes=chunk_scratch(chunks[0])
            + [pltpu.VMEM((2, TOP + 8, half), jnp.float32), pltpu.SemaphoreType.DMA((4,))],
        ),
        out_shape=jax.ShapeDtypeStruct(acc.shape, acc.dtype),
        input_output_aliases={3 + len(chunks): 0},
        compiler_params=params(),
        cost_estimate=estimate(14),
        name="fold_chunks",
    )(selection, pos, q, *chunks, acc)


def last_kernel(call, sel_ref, pos_ref, q_ref, *refs):
    n = 2
    chunks, (acc_ref, gain_ref, out_ref, k_ref, v_ref, chunk_ref, sem) = refs[:n], refs[n:]
    count = times_used(call, sel_ref, pos_ref)

    def finish(acc):
        out = acc[:HD] / acc[HD : HD + 1]
        out = out * lax.rsqrt(jnp.mean(out * out, axis=0, keepdims=True) + EPSILON)
        out_ref[...] = (out.T * gain_ref[...]).astype(jnp.bfloat16)

    @pl.when(count > 0)
    def _():
        place_chunks(call, sel_ref, pos_ref, chunks, chunk_ref, sem, k_ref, v_ref)
        finish(folded(q_ref[...], count, acc_ref[:TOP], acc_ref[TOP : TOP + 1], k_ref, v_ref)[0])

    @pl.when(count == 0)
    def _():
        finish(acc_ref[:TOP])


def fold_last(away, call, selection, pos, q, got, acc, gain):
    sources, _, rows, width = q.shape
    half = sources * rows
    chunks = call_chunks(call, got)
    return pl.pallas_call(
        functools.partial(last_kernel, call),
        grid_spec=pltpu.PrefetchScalarGridSpec(
            num_scalar_prefetch=2,
            grid=(1,),
            in_specs=[
                pl.BlockSpec((sources // 2, 2, rows, width), lambda i, sel, pos: (half_of(pos, away), 1, 0, 0)),
            ]
            + [pl.BlockSpec(memory_space=pl.ANY)] * len(chunks)
            + [
                pl.BlockSpec((TOP + 8, half), lambda i, sel, pos: (0, half_of(pos, away))),
                pl.BlockSpec((1, width), lambda i, sel, pos: (0, 0)),
            ],
            out_specs=pl.BlockSpec((half, width), lambda i, sel, pos: (0, 0)),
            scratch_shapes=chunk_scratch(chunks[0]),
        ),
        out_shape=jax.ShapeDtypeStruct((half, width), jnp.bfloat16),
        compiler_params=params(),
        cost_estimate=estimate(8),
        name="fold_last",
    )(selection, pos, q, *chunks, acc, gain)


def states_kernel(kv_ref, weight_ref, decay_ref, entering_ref, final_ref):
    spans = entering_ref.shape[0]
    state = jnp.zeros((HD, HD), jnp.float32)
    whole = jnp.ones((1, HD), jnp.float32)
    for s in range(spans):
        rows = pl.ds(s % SUB * CH, CH)
        entering_ref[s] = state
        k = kv_ref[s // SUB, 0, rows, :].astype(jnp.float32)
        v = kv_ref[s // SUB, 1, rows, :]
        weighted = (k * weight_ref[:, s : s + 1]).astype(jnp.bfloat16)
        inc = lax.dot_general(
            weighted, v, (((0,), (0,)), ((), ())), preferred_element_type=jnp.float32
        )
        state = decay_ref[s : s + 1, :] * state + inc
        whole = whole * decay_ref[s : s + 1, :]
    final_ref[:HD, :] = state
    final_ref[HD:, :] = jnp.broadcast_to(whole, (8, HD))


def states(kv, weight, decay):
    spans = decay.shape[0]
    return pl.pallas_call(
        states_kernel,
        out_shape=[
            jax.ShapeDtypeStruct((spans, HD, HD), jnp.float32),
            jax.ShapeDtypeStruct((HD + 8, HD), jnp.float32),
        ],
        compiler_params=params(),
        cost_estimate=estimate(2),
        name="span_states",
    )(kv, weight, decay)


def linear_kernel(q_ref, kv_ref, entering_ref, one_ref, two_ref, three_ref, cum_ref, cum_t_ref, lead_ref, gain_ref, out_ref):
    carried = two_ref[:HD, :] + two_ref[HD : HD + 1, :] * three_ref[:HD, :]
    carried = one_ref[:HD, :] + one_ref[HD : HD + 1, :] * carried
    spans = entering_ref.shape[0]
    r = lax.broadcasted_iota(jnp.int32, (CH, CH), 0)
    c = lax.broadcasted_iota(jnp.int32, (CH, CH), 1)
    causal = c <= r
    for s in range(spans):
        rows = pl.ds(s % SUB * CH, CH)
        q = q_ref[s // SUB, rows, :]
        k, v = (kv_ref[s // SUB, n, rows, :] for n in range(2))
        column = cum_t_ref[:, s : s + 1]
        gap = jnp.where(causal, column - cum_ref[s : s + 1, :], 0.0)
        damping = jnp.where(causal, jnp.exp(gap), 0.0)
        mixing = (dot_t(q, k) * damping).astype(jnp.bfloat16)
        inside = jnp.dot(mixing, v, preferred_element_type=jnp.float32)
        state = entering_ref[s] + lead_ref[s : s + 1, :] * carried
        high = state.astype(jnp.bfloat16)
        low = (state - high.astype(jnp.float32)).astype(jnp.bfloat16)
        across = jnp.dot(q, jnp.concatenate([high, low], axis=1), preferred_element_type=jnp.float32)
        out = inside + jnp.exp(column) * (across[:, :HD] + across[:, HD:])
        out_ref[s * CH : (s + 1) * CH, :] = (normalize(out) * gain_ref[...]).astype(jnp.bfloat16)


def linear(q, kv, entering, finals, cum, cum_t, lead, gain):
    spans = cum.shape[0]
    return pl.pallas_call(
        linear_kernel,
        out_shape=jax.ShapeDtypeStruct((spans * CH, HD), jnp.bfloat16),
        compiler_params=params(),
        cost_estimate=estimate(5),
        name="linear_heads",
    )(q, kv, entering, *finals, cum, cum_t, lead, gain)


def paired_device(queries, keys, values, log_decay, selection, out_gain):
    z, x = lax.axis_index("z"), lax.axis_index("x")
    pos = jnp.stack([z, x]).astype(jnp.int32)

    def to_heads(parts):
        return lax.all_to_all(parts, ("x", "y", "c"), 0, 0, tiled=True)

    def after(a, *earlier):
        return lax.optimization_barrier((a,) + earlier)[0]

    part_a = to_heads(first_pack(keys, values))
    front, kv_lin, q_lin = pack(queries, keys, values)
    swap = [(0, 1), (1, 0)]
    own_decay = lax.dynamic_index_in_dim(log_decay, x, 1, False)
    sent_decay = lax.dynamic_index_in_dim(log_decay, 1 - x, 1, False)
    got_decay = lax.ppermute(sent_decay, "x", swap)
    front = to_heads(after(front, part_a, got_decay))
    two, both = chosen(selection)
    early, late = (z == 2) & ~two, (z == 2) & ~both
    up = [(0, 1), (1, 2), (2, 3)]
    got, sent = [], []

    def go_up(*earlier):
        t = len(got)
        if t == 0:
            send = part_a
        elif t < 3:
            send = jnp.where(early, got[t - 1], after((front[:, :2], got[0])[t - 1], *earlier))
        elif t < 4:
            send = jnp.where(late, got[t - 1], after(got[t - 2], *earlier))
        else:
            send = after(got[t - 1], *earlier)
        sent.append(send)
        got.append(lax.ppermute(send, "z", up if t < 2 else up[1:] if t < 4 else up[2:]))

    def fold_in(call, acc, *earlier):
        return fold(call, selection, pos, front, got, after(acc, *earlier))

    gains = lax.dynamic_slice_in_dim(out_gain, x * 2 * HD, 2 * HD).reshape(2, 1, HD)
    go_up()
    go_up()
    kv_lin = to_heads(after(kv_lin, front))
    acc = own_block(front, after(part_a, sent[1]))
    acc = own_block(front, front, acc)
    decays = jnp.where(x == 0, jnp.stack([own_decay, got_decay]), jnp.stack([got_decay, own_decay]))
    cum = jnp.cumsum(decays.reshape(-1, CH), axis=1)
    ending = cum[:, -1]
    spans = cum.shape[0]
    weight = jnp.exp(ending[:, None] - cum).T
    decay = jnp.broadcast_to(jnp.exp(ending)[:, None], (spans, HD))
    lead = jnp.broadcast_to(jnp.exp(jnp.cumsum(ending) - ending)[:, None], (spans, HD))
    go_up(acc, weight, decay, lead, cum)
    acc = fold_in(1, acc, sent[2])
    entering, final = states(after(kv_lin, acc), weight, decay)
    finals = [lax.ppermute(final, "z", pairs) for pairs in (up, [(0, 2), (1, 3)], [(0, 3)])]
    q_lin = to_heads(after(q_lin, final))
    go_up(final)
    acc = fold_in(2, acc, sent[3])
    go_up(acc, *finals)
    entering = after(entering, acc)
    lin = linear(q_lin, kv_lin, entering, finals, cum, cum.T, lead, gains[0])
    acc = fold_in(3, after(acc, lin))
    rows = lin.shape[0] // 2
    lin_own = lax.dynamic_slice_in_dim(lin, x * rows, rows)
    lin_got = lax.ppermute(lax.dynamic_slice_in_dim(lin, (1 - x) * rows, rows), "x", swap)

    att_away = fold_last(True, 4, selection, pos, front, got, acc, gains[1])
    att_got = lax.ppermute(att_away, "x", swap)
    att_own = fold_last(False, 4, selection, pos, front, got, acc, gains[1])
    return jnp.where(
        x == 0,
        jnp.concatenate([lin_own, att_own, lin_got, att_got], axis=1),
        jnp.concatenate([lin_got, att_got, lin_own, att_own], axis=1),
    )


def solution(mesh):
    args = (P(("seq", "head"), None),) * 3 + (P("seq", "head"), P(), P("head"))
    if mesh.shape["seq"] == 8 and mesh.shape["head"] == 4:
        fine = jax.sharding.Mesh(mesh.devices.reshape(4, 2, 2, 2), ("z", "x", "y", "c"))
        everywhere = P(("z", "x", "y", "c"), None)
        return jax.shard_map(
            paired_device,
            mesh=fine,
            in_specs=(everywhere,) * 3 + (P(("z", "x"), ("y", "c")), P(), P(("y", "c"))),
            out_specs=P(("z", "x"), ("y", "c")),
            check_vma=False,
        )
    return jax.shard_map(
        per_device, mesh=mesh, in_specs=args, out_specs=P("seq", "head"), check_vma=False
    )
```

```python
import functools

import jax
import jax.numpy as jnp
from jax import lax
from jax.experimental import pallas as pl
from jax.experimental.pallas import tpu as pltpu
from jax.sharding import PartitionSpec as P

HD = 128
BLK = 4096
TILE = 1024
CH = 128


EPSILON = 1e-06
NEGATIVE = -1e30
HIGHEST = lax.Precision.HIGHEST
VMEM_LIMIT = 56 << 20


def carried_in(part, axis, combine, identity):
    place = lax.axis_index(axis)
    gathered = jax.tree.map(lambda a: lax.all_gather(a, axis), part)
    state = jax.tree.map(lambda a, e: jnp.zeros_like(a) + jnp.asarray(e, a.dtype), part, identity)

    def one(turn, state):
        return combine(
            state, jax.tree.map(lambda a: lax.dynamic_index_in_dim(a, turn, 0, False), gathered)
        )

    return lax.fori_loop(0, place, one, state)


def within_spans(query_lin, key_lin, value_lin, log_decay, span):
    rows, record_entries, width = query_lin.shape
    count = rows // span
    probe_segments = query_lin.reshape(count, span, record_entries, width)
    key_spans = key_lin.reshape(count, span, record_entries, width)
    value_spans = value_lin.reshape(count, span, record_entries, width)
    running = jnp.cumsum(log_decay.reshape(count, span, record_entries), axis=1)
    by_line = jnp.transpose(running, (0, 2, 1))
    causal = jnp.arange(span)[:, None] >= jnp.arange(span)[None, :]
    stride_gap = jnp.where(causal, by_line[:, :, :, None] - by_line[:, :, None, :], 0.0)
    damping = jnp.where(causal, jnp.exp(stride_gap), 0.0)
    scores = jnp.einsum(
        "ctld,csld->clts", probe_segments, key_spans, preferred_element_type=jnp.float32
    )
    mixing = (scores * damping).astype(jnp.bfloat16)
    inside = jnp.einsum("clts,csld->ctld", mixing, value_spans, preferred_element_type=jnp.float32)
    ending = running[:, -1, :]
    weighted_keys = (
        key_spans.astype(jnp.float32) * jnp.exp(ending[:, None, :] - running)[..., None]
    ).astype(jnp.bfloat16)
    increments = jnp.einsum(
        "ctld,ctle->clde", weighted_keys, value_spans, preferred_element_type=jnp.float32
    )

    def advance(state, inputs):
        decay_sum, increment = inputs
        return (jnp.exp(decay_sum)[:, None, None] * state + increment, state)

    final_state, entering = lax.scan(
        advance, jnp.zeros((record_entries, width, width), jnp.float32), (ending, increments)
    )
    weighted_queries = probe_segments.astype(jnp.float32) * jnp.exp(running)[..., None]
    across = jnp.einsum("ctld,clde->ctle", weighted_queries, entering, precision=HIGHEST)
    return (inside + across, weighted_queries, ending, final_state)


def attend_tiles(query, key_tiles, payload_blocks, query_pos, slot_open, per_slot):
    rows, record_entries, width = query.shape
    tile_len = key_tiles.shape[1]
    scale = width ** (-0.5)

    def tile_step(tile, carry):
        best, total, accum = carry
        slot = tile // per_slot
        key_pos = tile % per_slot * tile_len + jnp.arange(tile_len)
        key_tile = lax.dynamic_index_in_dim(key_tiles, tile, 0, keepdims=False)
        value_tile = lax.dynamic_index_in_dim(payload_blocks, tile, 0, keepdims=False)
        causal = key_pos[None, :] <= query_pos[:, None]
        allowed = jnp.where(slot == 0, causal, slot_open[slot])
        scores = (
            jnp.einsum("ild,jld->lij", query, key_tile, preferred_element_type=jnp.float32) * scale
        )
        masked = jnp.where(allowed[None], scores, NEGATIVE)
        tile_max = jnp.max(masked, axis=2)
        probs = jnp.where(allowed[None], jnp.exp(masked - tile_max[:, :, None]), 0.0).astype(
            jnp.bfloat16
        )
        tile_sum = jnp.sum(probs, axis=2, dtype=jnp.float32)
        tile_out = jnp.einsum("lij,jld->ild", probs, value_tile, preferred_element_type=jnp.float32)
        peak = jnp.maximum(best, tile_max)
        keep = jnp.exp(best - peak)
        fresh = jnp.exp(tile_max - peak)
        total = total * keep + tile_sum * fresh
        accum = accum * keep.T[:, :, None] + tile_out * fresh.T[:, :, None]
        return (peak, total, accum)

    start = (
        jnp.full((record_entries, rows), NEGATIVE, jnp.float32),
        jnp.zeros((record_entries, rows), jnp.float32),
        jnp.zeros((rows, record_entries, width), jnp.float32),
    )
    best, total, accum = lax.fori_loop(0, key_tiles.shape[0], tile_step, start)
    return accum / total.T[:, :, None]


def request_table(selection, group, seq_count):
    dest_block = jnp.arange(seq_count) // group
    chosen = jnp.take(selection, dest_block, axis=0)
    return jnp.transpose(chosen)[:, None, :] * group + jnp.arange(group)[None, :, None]


def normalize(heads):
    return heads * lax.rsqrt(jnp.mean(heads * heads, axis=-1, keepdims=True) + EPSILON)


def per_device(queries, keys, values, log_decay, selection, out_gain):
    queries, keys, values = (
        lax.all_to_all(queries, "head", split_axis=1, concat_axis=0, tiled=True),
        lax.all_to_all(keys, "head", split_axis=1, concat_axis=0, tiled=True),
        lax.all_to_all(values, "head", split_axis=1, concat_axis=0, tiled=True),
    )
    rows = queries.shape[0]
    width = HD
    pairs = queries.shape[1] // (2 * width)
    query_pairs = queries.reshape(rows, pairs, 2, width)
    paired_keys = keys.reshape(rows, pairs, 2, width)
    paired_values = values.reshape(rows, pairs, 2, width)
    linear_part, weighted_queries, ending, final_state = within_spans(
        query_pairs[:, :, 0], paired_keys[:, :, 0], paired_values[:, :, 0], log_decay, CH
    )
    total_decay = jnp.sum(ending, axis=0)

    def chain(earlier, later):
        return (earlier[0] + later[0], jnp.exp(later[0])[:, None, None] * earlier[1] + later[1])

    leading_decay, carried = carried_in(
        (total_decay, final_state),
        "seq",
        chain,
        (jnp.zeros_like(total_decay), jnp.zeros_like(final_state)),
    )
    span_start = jnp.cumsum(ending, axis=0) - ending
    shifted = weighted_queries * jnp.exp(span_start)[:, None, :, None]
    correction = jnp.einsum("ctld,lde->ctle", shifted, carried, precision=HIGHEST)
    linear_out = (linear_part + correction).reshape(rows, pairs, width)
    seq_count = lax.axis_size("seq")
    position = lax.axis_index("seq")
    group = BLK // rows
    block_index = position // group
    rank = position % group
    piece_rows = rows // seq_count
    query_moba = query_pairs[:, :, 1]
    key_moba = paired_keys[:, :, 1]
    value_moba = paired_values[:, :, 1]
    spread_keys, spread_values = (
        lax.all_to_all(
            key_moba.reshape(seq_count, piece_rows, pairs, width),
            "seq",
            split_axis=0,
            concat_axis=0,
            tiled=True,
        ),
        lax.all_to_all(
            value_moba.reshape(seq_count, piece_rows, pairs, width),
            "seq",
            split_axis=0,
            concat_axis=0,
            tiled=True,
        ),
    )
    table = request_table(selection, group, seq_count)
    block_keys, block_values = (
        lax.all_to_all(
            jnp.take(spread_keys, table, axis=0), "seq", split_axis=2, concat_axis=2, tiled=True
        ),
        lax.all_to_all(
            jnp.take(spread_values, table, axis=0), "seq", split_axis=2, concat_axis=2, tiled=True
        ),
    )
    block_keys = block_keys.reshape(3, BLK, pairs, width)
    block_values = block_values.reshape(3, BLK, pairs, width)
    per_slot = BLK // TILE
    key_tiles = block_keys.reshape(3 * per_slot, TILE, pairs, width)
    payload_blocks = block_values.reshape(3 * per_slot, TILE, pairs, width)
    chosen = jnp.take(selection, block_index, axis=0)
    slot_open = jnp.concatenate([jnp.ones((1,), jnp.bool_), chosen[1:] != block_index])
    query_pos = rank * rows + jnp.arange(rows)
    attended = attend_tiles(query_moba, key_tiles, payload_blocks, query_pos, slot_open, per_slot)
    both = jnp.stack([normalize(linear_out), normalize(attended)], axis=2).reshape(
        rows, pairs * 2 * width
    )
    return (both * out_gain[None, :]).astype(jnp.bfloat16)


SUB = 4
QUARTER = 128
SUMS = 16
TOP = HD + SUMS
SPEED = 2e7
LOG2E = 1.4426950408889634


def dot_t(a, b):
    return lax.dot_general(a, b, (((1,), (1,)), ((), ())), preferred_element_type=jnp.float32)


def scaled(q):
    wide = q.astype(jnp.float32) * (HD ** (-0.5) * LOG2E)
    high = wide.astype(jnp.bfloat16)
    return jnp.concatenate([high, (wide - high.astype(jnp.float32)).astype(jnp.bfloat16)], axis=1)


def place(k, v, k_ref, v_ref, at):
    rows = k.shape[0]
    k_ref[at : at + rows, :] = jnp.concatenate([k, k], axis=1)
    for i in range(0, rows, QUARTER):
        v_ref[:HD, at + i : at + i + QUARTER] = v[i : i + QUARTER, :]
    v_ref[HD:, at : at + rows] = jnp.ones((SUMS, rows), jnp.bfloat16)


def quarters(v):
    return jnp.concatenate([v[i : i + QUARTER].T for i in range(0, v.shape[0], QUARTER)], axis=0)


def estimate(us, transcendentals=0):
    return pl.CostEstimate(flops=int(us * SPEED), bytes_accessed=1 << 20, transcendentals=transcendentals)


def params(limit=VMEM_LIMIT):
    return pltpu.CompilerParams(vmem_limit_bytes=limit)


def taker(p):
    return 2 * (p % 4) + p // 4


def first_pack_kernel(q_ref, k_ref, v_ref, out_ref):
    rows = k_ref.shape[0]
    for p in range(8):
        at = pl.ds((2 * taker(p) + 1) * HD, HD)
        out_ref[p, 0] = k_ref[:, at]
        out_ref[p, 1] = quarters(v_ref[:, at])
        out_ref[p, 2] = q_ref[:rows, at]
        out_ref[p, 3] = q_ref[rows:, at]


def first_pack(queries, keys, values):
    rows, width = keys.shape[0] // 2, keys.shape[1]
    half = pl.BlockSpec((rows, width), lambda i: (0, 0))
    return pl.pallas_call(
        first_pack_kernel,
        grid=(1,),
        in_specs=[pl.BlockSpec(queries.shape, lambda i: (0, 0)), half, half],
        out_specs=pl.BlockSpec((8, 4, rows, HD), lambda i: (0, 0, 0, 0)),
        out_shape=jax.ShapeDtypeStruct((8, 4, rows, HD), jnp.bfloat16),
        compiler_params=params(),
        cost_estimate=estimate(3),
        name="pack_first",
    )(queries, keys, values)


def pack_kernel(q_ref, k_ref, v_ref, b_ref, kv_ref, q_out):
    half = b_ref.shape[2]
    for n in range(2):
        b_ref[n, 0] = k_ref[half:, (2 * n + 1) * HD : (2 * n + 2) * HD]
        b_ref[n, 1] = quarters(v_ref[half:, (2 * n + 1) * HD : (2 * n + 2) * HD])
        for m, ref in enumerate((k_ref, v_ref)):
            kv_ref[n, m] = ref[:, 2 * n * HD : (2 * n + 1) * HD]
        q_out[n] = q_ref[:, 2 * n * HD : (2 * n + 1) * HD]


def pack(queries, keys, values):
    tokens = keys.shape[0]
    spec = pl.BlockSpec((tokens, 4 * HD), lambda j: (0, j))
    shapes = [(2, 4, 2, tokens // 2, HD), (2, 4, 2, tokens, HD), (2, 4, tokens, HD)]
    out = pl.pallas_call(
        pack_kernel,
        grid=(4,),
        in_specs=[spec, spec, spec],
        out_specs=[pl.BlockSpec((2, None) + shape[2:], lambda j, n=len(shape): (0, j) + (0,) * (n - 2)) for shape in shapes],
        out_shape=[jax.ShapeDtypeStruct(shape, jnp.bfloat16) for shape in shapes],
        compiler_params=params(),
        cost_estimate=estimate(5),
        name="pack_rest",
    )(queries, keys, values)
    return [a.reshape((8,) + a.shape[2:]) for a in out]


def own_kernel(first, q_ref, kv_ref, *refs):
    if first:
        acc_ref, k_ref, v_ref = refs
    else:
        acc_in, acc_ref, k_ref, v_ref = refs
    sources, _, rows, width = kv_ref.shape
    for p in range(sources):
        place(kv_ref[p, 0], kv_ref[p, 1], k_ref, v_ref, p * rows)
    key = lax.broadcasted_iota(jnp.int32, (rows, 2 * rows), 0)
    query = lax.broadcasted_iota(jnp.int32, (rows, 2 * rows), 1)
    causal = key + (0 if first else rows) <= query
    for i in range(sources):
        columns = slice(i * 2 * rows, (i + 1) * 2 * rows)
        q = scaled(q_ref[i].reshape(2 * rows, width))
        s = jnp.where(causal, dot_t(k_ref[i * rows : (i + 1) * rows, :], q), NEGATIVE)
        m = jnp.max(s, axis=0, keepdims=True)
        if not first:
            old = acc_in[TOP : TOP + 1, columns]
            m = jnp.maximum(old, m)
        if i:
            before = dot_t(k_ref[: i * rows, :], q)
            m = jnp.maximum(m, jnp.max(before, axis=0, keepdims=True))
        prob = jnp.exp2(s - m).astype(jnp.bfloat16)
        acc = jnp.dot(v_ref[:, i * rows : (i + 1) * rows], prob, preferred_element_type=jnp.float32)
        if i:
            prob = jnp.exp2(before - m).astype(jnp.bfloat16)
            acc += jnp.dot(v_ref[:, : i * rows], prob, preferred_element_type=jnp.float32)
        if not first:
            acc += acc_in[:TOP, columns] * jnp.exp2(old - m)
        acc_ref[:TOP, columns] = acc
        acc_ref[TOP:, columns] = jnp.broadcast_to(m, (8, 2 * rows))


def own_block(q, kv, acc=None):
    sources, _, rows, width = q.shape
    tokens = sources * rows * 2
    acc_spec = pl.BlockSpec((TOP + 8, tokens), lambda i: (0, 0))
    return pl.pallas_call(
        functools.partial(own_kernel, acc is None),
        grid=(1,),
        in_specs=[
            pl.BlockSpec((sources, 2, rows, width), lambda i: (0, 1, 0, 0)),
            pl.BlockSpec((sources, 2, rows, width), lambda i: (0, 0, 0, 0)),
        ]
        + ([] if acc is None else [acc_spec]),
        out_specs=acc_spec,
        scratch_shapes=[
            pltpu.VMEM((tokens // 2, 2 * width), jnp.bfloat16),
            pltpu.VMEM((TOP, tokens // 2), jnp.bfloat16),
        ],
        out_shape=jax.ShapeDtypeStruct((TOP + 8, tokens), jnp.float32),
        compiler_params=params(),
        cost_estimate=estimate(11),
        name="own_block",
    )(q, kv, *([] if acc is None else [acc]))


def half_of(pos_ref, away):
    return 1 - pos_ref[1] if away else pos_ref[1]


def chosen(sel_ref):
    two = (sel_ref[3, 1] == 2) | (sel_ref[3, 2] == 2)
    return two, two & ((sel_ref[3, 1] == 1) | (sel_ref[3, 2] == 1))


def chunk_now(call, sel_ref, pos_ref):
    two, both = chosen(sel_ref)
    return (pos_ref[0] == 3) & ((~two | ~both) if call > 2 else ~two)


def times_used(call, sel_ref, pos_ref):
    z = pos_ref[0]
    two, both = chosen(sel_ref)

    def third(step):
        return (2, jnp.where(two, 2, 1), 1, jnp.where(both, 1, 0), jnp.where(both, -1, 0))[step]

    before = jnp.where(
        z == 1, (0, 0, -1, -1)[call - 1], jnp.where(z == 2, (1, 1, 0, 0)[call - 1], third(call - 1))
    )
    block = jnp.where(chunk_now(call, sel_ref, pos_ref), third(call), before)
    block = jnp.where(z == 0, -1, block)
    return (sel_ref[z, 1] == block).astype(jnp.int32) + (sel_ref[z, 2] == block).astype(jnp.int32)


def place_chunks(call, sel_ref, pos_ref, chunks, chunk_ref, sem, k_ref, v_ref):
    now = chunk_now(call, sel_ref, pos_ref)
    for n, cond in enumerate((~now, now)):

        @pl.when(cond)
        def _():
            copy = pltpu.make_async_copy(chunks[n], chunk_ref, sem)
            copy.start()
            copy.wait()

    sources, _, rows, _ = chunk_ref.shape
    for p in range(sources):
        place(chunk_ref[p, 0], chunk_ref[p, 1], k_ref, v_ref, p * rows)


def folded(q, count, acc, old, k_ref, v_ref):
    s = dot_t(k_ref[...], scaled(q.reshape(-1, HD)))
    m = jnp.maximum(old, jnp.max(s, axis=0, keepdims=True))
    prob = jnp.exp2(s - m).astype(jnp.bfloat16)
    acc = acc * jnp.exp2(old - m) + count.astype(jnp.float32) * jnp.dot(
        v_ref[...], prob, preferred_element_type=jnp.float32
    )
    return acc, m


def fold_kernel(call, sel_ref, pos_ref, q_ref, *refs):
    n = 2
    chunks, (acc_in, acc_out, k_ref, v_ref, chunk_ref, chunk_sem, acc_ref, sem) = refs[:n], refs[n:]
    count = times_used(call, sel_ref, pos_ref)
    sources, _, rows, width = q_ref.shape
    half = sources * rows

    @pl.when(count > 0)
    def _():
        def copies(out):
            for h in range(2):
                part = pl.ds(h * half, half)
                there, here = (acc_out if out else acc_in).at[:, part], acc_ref.at[h]
                yield pltpu.make_async_copy(*((here, there) if out else (there, here)), sem.at[2 * out + h])

        fetch, store = list(copies(0)), list(copies(1))
        for copy in fetch:
            copy.start()
        place_chunks(call, sel_ref, pos_ref, chunks, chunk_ref, chunk_sem, k_ref, v_ref)
        for h in range(2):
            fetch[h].wait()
            q = q_ref[h * sources // 2 : (h + 1) * sources // 2]
            acc, m = folded(q, count, acc_ref[h, :TOP], acc_ref[h, TOP : TOP + 1], k_ref, v_ref)
            acc_ref[h, :TOP] = acc
            acc_ref[h, TOP:] = jnp.broadcast_to(m, (8, half))
            store[h].start()
        for copy in store:
            copy.wait()


def chunk_scratch(chunk):
    keys = chunk.shape[0] * chunk.shape[2]
    return [
        pltpu.VMEM((keys, 2 * HD), jnp.bfloat16),
        pltpu.VMEM((TOP, keys), jnp.bfloat16),
        pltpu.VMEM(chunk.shape, chunk.dtype),
        pltpu.SemaphoreType.DMA,
    ]


def call_chunks(call, got):
    return got[call - 1 : call + 1]


def fold(call, selection, pos, q, got, acc):
    sources, _, rows, width = q.shape
    half = sources * rows
    chunks = call_chunks(call, got)
    anywhere = pl.BlockSpec(memory_space=pl.ANY)
    return pl.pallas_call(
        functools.partial(fold_kernel, call),
        grid_spec=pltpu.PrefetchScalarGridSpec(
            num_scalar_prefetch=2,
            grid=(1,),
            in_specs=[pl.BlockSpec((sources, 2, rows, width), lambda i, sel, pos: (0, 1, 0, 0))]
            + [anywhere] * (len(chunks) + 1),
            out_specs=anywhere,
            scratch_shapes=chunk_scratch(chunks[0])
            + [pltpu.VMEM((2, TOP + 8, half), jnp.float32), pltpu.SemaphoreType.DMA((4,))],
        ),
        out_shape=jax.ShapeDtypeStruct(acc.shape, acc.dtype),
        input_output_aliases={3 + len(chunks): 0},
        compiler_params=params(),
        cost_estimate=estimate(14),
        name="fold_chunks",
    )(selection, pos, q, *chunks, acc)


def last_kernel(call, sel_ref, pos_ref, q_ref, *refs):
    n = 2
    chunks, (acc_ref, gain_ref, out_ref, k_ref, v_ref, chunk_ref, sem) = refs[:n], refs[n:]
    count = times_used(call, sel_ref, pos_ref)

    def finish(acc):
        out = acc[:HD] / acc[HD : HD + 1]
        out = out * lax.rsqrt(jnp.mean(out * out, axis=0, keepdims=True) + EPSILON)
        out_ref[...] = (out.T * gain_ref[...]).astype(jnp.bfloat16)

    @pl.when(count > 0)
    def _():
        place_chunks(call, sel_ref, pos_ref, chunks, chunk_ref, sem, k_ref, v_ref)
        finish(folded(q_ref[...], count, acc_ref[:TOP], acc_ref[TOP : TOP + 1], k_ref, v_ref)[0])

    @pl.when(count == 0)
    def _():
        finish(acc_ref[:TOP])


def fold_last(away, call, selection, pos, q, got, acc, gain):
    sources, _, rows, width = q.shape
    half = sources * rows
    chunks = call_chunks(call, got)
    return pl.pallas_call(
        functools.partial(last_kernel, call),
        grid_spec=pltpu.PrefetchScalarGridSpec(
            num_scalar_prefetch=2,
            grid=(1,),
            in_specs=[
                pl.BlockSpec((sources // 2, 2, rows, width), lambda i, sel, pos: (half_of(pos, away), 1, 0, 0)),
            ]
            + [pl.BlockSpec(memory_space=pl.ANY)] * len(chunks)
            + [
                pl.BlockSpec((TOP + 8, half), lambda i, sel, pos: (0, half_of(pos, away))),
                pl.BlockSpec((1, width), lambda i, sel, pos: (0, 0)),
            ],
            out_specs=pl.BlockSpec((half, width), lambda i, sel, pos: (0, 0)),
            scratch_shapes=chunk_scratch(chunks[0]),
        ),
        out_shape=jax.ShapeDtypeStruct((half, width), jnp.bfloat16),
        compiler_params=params(),
        cost_estimate=estimate(8),
        name="fold_last",
    )(selection, pos, q, *chunks, acc, gain)


def states_kernel(kv_ref, weight_ref, decay_ref, entering_ref, final_ref):
    spans = entering_ref.shape[0]
    state = jnp.zeros((HD, HD), jnp.float32)
    whole = jnp.ones((1, HD), jnp.float32)
    for s in range(spans):
        rows = pl.ds(s % SUB * CH, CH)
        entering_ref[s] = state
        k = kv_ref[s // SUB, 0, rows, :].astype(jnp.float32)
        v = kv_ref[s // SUB, 1, rows, :]
        weighted = (k * weight_ref[:, s : s + 1]).astype(jnp.bfloat16)
        inc = lax.dot_general(
            weighted, v, (((0,), (0,)), ((), ())), preferred_element_type=jnp.float32
        )
        state = decay_ref[s : s + 1, :] * state + inc
        whole = whole * decay_ref[s : s + 1, :]
    final_ref[:HD, :] = state
    final_ref[HD:, :] = jnp.broadcast_to(whole, (8, HD))


def states(kv, weight, decay):
    spans = decay.shape[0]
    return pl.pallas_call(
        states_kernel,
        out_shape=[
            jax.ShapeDtypeStruct((spans, HD, HD), jnp.float32),
            jax.ShapeDtypeStruct((HD + 8, HD), jnp.float32),
        ],
        compiler_params=params(),
        cost_estimate=estimate(2),
        name="span_states",
    )(kv, weight, decay)


def linear_kernel(q_ref, kv_ref, entering_ref, one_ref, two_ref, three_ref, cum_ref, cum_t_ref, lead_ref, gain_ref, out_ref):
    carried = two_ref[:HD, :] + two_ref[HD : HD + 1, :] * three_ref[:HD, :]
    carried = one_ref[:HD, :] + one_ref[HD : HD + 1, :] * carried
    spans = entering_ref.shape[0]
    r = lax.broadcasted_iota(jnp.int32, (CH, CH), 0)
    c = lax.broadcasted_iota(jnp.int32, (CH, CH), 1)
    causal = c <= r
    for s in range(spans):
        rows = pl.ds(s % SUB * CH, CH)
        q = q_ref[s // SUB, rows, :]
        k, v = (kv_ref[s // SUB, n, rows, :] for n in range(2))
        column = cum_t_ref[:, s : s + 1]
        gap = jnp.where(causal, column - cum_ref[s : s + 1, :], 0.0)
        damping = jnp.where(causal, jnp.exp(gap), 0.0)
        mixing = (dot_t(q, k) * damping).astype(jnp.bfloat16)
        inside = jnp.dot(mixing, v, preferred_element_type=jnp.float32)
        state = entering_ref[s] + lead_ref[s : s + 1, :] * carried
        high = state.astype(jnp.bfloat16)
        low = (state - high.astype(jnp.float32)).astype(jnp.bfloat16)
        across = jnp.dot(q, jnp.concatenate([high, low], axis=1), preferred_element_type=jnp.float32)
        out = inside + jnp.exp(column) * (across[:, :HD] + across[:, HD:])
        out_ref[s * CH : (s + 1) * CH, :] = (normalize(out) * gain_ref[...]).astype(jnp.bfloat16)


def linear(q, kv, entering, finals, cum, cum_t, lead, gain):
    spans = cum.shape[0]
    return pl.pallas_call(
        linear_kernel,
        out_shape=jax.ShapeDtypeStruct((spans * CH, HD), jnp.bfloat16),
        compiler_params=params(),
        cost_estimate=estimate(5),
        name="linear_heads",
    )(q, kv, entering, *finals, cum, cum_t, lead, gain)


def assemble_kernel(pos_ref, lin_own, att_own, lin_got, att_got, out_ref):
    for x in range(2):

        @pl.when(pos_ref[1] == x)
        def _():
            for n, ref in enumerate((lin_own, att_own)):
                out_ref[:, (2 * x + n) * HD : (2 * x + n + 1) * HD] = ref[...]
            for n, ref in enumerate((lin_got, att_got)):
                out_ref[:, (2 - 2 * x + n) * HD : (3 - 2 * x + n) * HD] = ref[...]


def assemble(pos, *heads):
    tokens, width = heads[0].shape
    rows = tokens // 2
    return pl.pallas_call(
        assemble_kernel,
        grid_spec=pltpu.PrefetchScalarGridSpec(
            num_scalar_prefetch=1,
            grid=(2,),
            in_specs=[pl.BlockSpec((rows, width), lambda i, pos: (i, 0))] * 4,
            out_specs=pl.BlockSpec((rows, 4 * width), lambda i, pos: (i, 0)),
        ),
        out_shape=jax.ShapeDtypeStruct((tokens, 4 * width), heads[0].dtype),
        compiler_params=params(),
        cost_estimate=estimate(2),
        name="side_by_side",
    )(pos, *heads)


def paired_device(queries, keys, values, log_decay, selection, out_gain):
    z, x = lax.axis_index("z"), lax.axis_index("x")
    pos = jnp.stack([z, x]).astype(jnp.int32)

    def to_heads(parts):
        return lax.all_to_all(parts, ("x", "y", "c"), 0, 0, tiled=True)

    def after(a, *earlier):
        return lax.optimization_barrier((a,) + earlier)[0]

    front = to_heads(first_pack(queries, keys, values))
    part_b, kv_lin, q_lin = pack(queries, keys, values)
    part_a = after(front, part_b)[:, :2]
    swap = [(0, 1), (1, 0)]
    own_decay = lax.dynamic_index_in_dim(log_decay, x, 1, False)
    sent_decay = lax.dynamic_index_in_dim(log_decay, 1 - x, 1, False)
    got_decay = lax.ppermute(sent_decay, "x", swap)
    part_b = to_heads(after(part_b, part_a, got_decay))
    two, both = chosen(selection)
    early, late = (z == 2) & ~two, (z == 2) & ~both
    up = [(0, 1), (1, 2), (2, 3)]
    got, sent = [], []

    def go_up(*earlier):
        t = len(got)
        if t == 0:
            send = part_a
        elif t < 3:
            send = jnp.where(early, got[t - 1], after((part_b, got[0])[t - 1], *earlier))
        elif t < 4:
            send = jnp.where(late, got[t - 1], after(got[t - 2], *earlier))
        else:
            send = after(got[t - 1], *earlier)
        sent.append(send)
        got.append(lax.ppermute(send, "z", up if t < 2 else up[1:] if t < 4 else up[2:]))

    def fold_in(call, acc, *earlier):
        return fold(call, selection, pos, front, got, after(acc, *earlier))

    gains = lax.dynamic_slice_in_dim(out_gain, x * 2 * HD, 2 * HD).reshape(2, 1, HD)
    go_up()
    acc = own_block(front, front)
    kv_lin = to_heads(after(kv_lin, acc))
    go_up(acc)
    acc = own_block(front, part_b, after(acc, sent[1]))
    decays = jnp.where(x == 0, jnp.stack([own_decay, got_decay]), jnp.stack([got_decay, own_decay]))
    cum = jnp.cumsum(decays.reshape(-1, CH), axis=1)
    ending = cum[:, -1]
    spans = cum.shape[0]
    weight = jnp.exp(ending[:, None] - cum).T
    decay = jnp.broadcast_to(jnp.exp(ending)[:, None], (spans, HD))
    lead = jnp.broadcast_to(jnp.exp(jnp.cumsum(ending) - ending)[:, None], (spans, HD))
    entering, final = states(after(kv_lin, acc), weight, decay)
    finals = [lax.ppermute(final, "z", pairs) for pairs in (up, [(0, 2), (1, 3)], [(0, 3)])]
    q_lin = to_heads(after(q_lin, final))
    go_up(acc, final, lead, cum)
    acc = fold_in(1, acc, sent[2])
    go_up(acc, *finals)
    acc = fold_in(2, acc, sent[3])
    go_up(acc)
    entering = after(entering, acc)
    lin = linear(q_lin, kv_lin, entering, finals, cum, cum.T, lead, gains[0])
    acc = fold_in(3, after(acc, lin))
    rows = lin.shape[0] // 2
    lin_own = lax.dynamic_slice_in_dim(lin, x * rows, rows)
    lin_got = lax.ppermute(lax.dynamic_slice_in_dim(lin, (1 - x) * rows, rows), "x", swap)

    att_away = fold_last(True, 4, selection, pos, front, got, acc, gains[1])
    att_got = lax.ppermute(att_away, "x", swap)
    att_own = fold_last(False, 4, selection, pos, front, got, acc, gains[1])
    return assemble(pos, lin_own, att_own, lin_got, att_got)


def solution(mesh):
    args = (P(("seq", "head"), None),) * 3 + (P("seq", "head"), P(), P("head"))
    if mesh.shape["seq"] == 8 and mesh.shape["head"] == 4:
        fine = jax.sharding.Mesh(mesh.devices.reshape(4, 2, 2, 2), ("z", "x", "y", "c"))
        everywhere = P(("z", "x", "y", "c"), None)
        return jax.shard_map(
            paired_device,
            mesh=fine,
            in_specs=(everywhere,) * 3 + (P(("z", "x"), ("y", "c")), P(), P(("y", "c"))),
            out_specs=P(("z", "x"), ("y", "c")),
            check_vma=False,
        )
    return jax.shard_map(
        per_device, mesh=mesh, in_specs=args, out_specs=P("seq", "head"), check_vma=False
    )
```
